512 devices in a mesh: group: 8 (over x, core), member: 64 (over y, z).
Axes of the slice: x: 4, y: 8, z: 8, core: 2. Of those that a mesh axis runs over, the one named last changes fastest.
Arguments:
- features: bfloat16 [131072, 256], P(('group', 'member')), may hold values from -6 to 6
- neighbours: int32 [131072, 10], P(('group', 'member')), may hold values from 0 to 3327
- send_rows: int32 [32768, 16], P(('group', 'member')), may hold values from 0 to 255
- block_counts: int32 [32768], P(('group', 'member')), may hold values from 1 to 16, as said below
- hub_rows: int32 [512, 4], P(('group', 'member')), may hold values from 0 to 255
- w_self: bfloat16 [256, 256], replicated, may hold values from -0.375 to 0.375
- w_nbr: bfloat16 [256, 256], replicated, may hold values from -0.375 to 0.375
- cotangent: bfloat16 [131072, 256], P(('group', 'member')), may hold values from -6 to 6
Outputs:
- grad_self: float32 [256, 256], replicated
- grad_nbr: float32 [256, 256], replicated
- grad_features: bfloat16 [131072, 256], P(('group', 'member'))
The draws below stay inside these ranges and needn't reach their ends.
Inputs may be any that keep to these rules, and one draw needn't show every extreme that they name: `block_counts`: entry pair of every fourth pair (pair % 4 == 0) is exactly 16.
All inputs are finite; a program needn't handle non-finite values.
Results may differ from the reference program's by a relative error of at most 0.005.
Values may be sent and summed in bfloat16 or wider, within the bound.
No kernel may reach another device: no remote copies, remote signals or barrier semaphores. Data moves between devices by JAX's collectives and lax.ppermute only.
A program may use at most 64 MiB of HBM per device.

```python
import math
import jax
import jax.numpy as jnp

D = 256
NODE_DEV = 256
FANOUT = 10
BLOCK = 16
HUB_DEV = 4
NODES = 131072
OWNERS = 512
SENDS = 32768
TABLE = 3328
N_GROUP = 8
N_MEMBER = 64


def draw_block_counts(key, part):
    key = jax.random.fold_in(key, 7)
    drawn = jax.random.randint(key, (SENDS,), 1, BLOCK + 1)
    return jnp.where(jnp.arange(SENDS) % 4 == 0, BLOCK, drawn).astype(jnp.int32)


def draw_neighbours(key, part):
    key = jax.random.fold_in(key, 11)
    shape = (NODES, FANOUT)
    kind_key, local_key, border_key, pick_key, far_key, hub_key = jax.random.split(key, 6)
    kind = jax.random.randint(kind_key, shape, 0, 3)
    local_pick = jax.random.randint(local_key, shape, 0, NODE_DEV)
    border_pick = NODE_DEV + jax.random.randint(border_key, shape, 0, N_MEMBER * BLOCK)
    device = (jnp.arange(NODES, dtype=jnp.int32) // NODE_DEV)[:, None]
    partner = jax.random.randint(pick_key, shape, 0, 4)
    anywhere = jax.random.randint(far_key, shape, 0, OWNERS)
    offset = jnp.where(partner == 0, OWNERS // 2, jnp.where(partner == 1, 1, jnp.where(partner == 2, OWNERS - 1, anywhere)))
    owner = (device + offset) % OWNERS
    hub_slot = jax.random.randint(hub_key, shape, 0, HUB_DEV)
    hub_pick = NODE_DEV + N_MEMBER * BLOCK + owner * HUB_DEV + hub_slot
    chosen = jnp.where(kind == 0, local_pick, jnp.where(kind == 1, border_pick, hub_pick))
    chosen = chosen.at[0, 0].set(0)
    chosen = chosen.at[1, 0].set(TABLE - 1)
    return chosen.astype(jnp.int32)


def set_ends(result, rng, least, top_value):
    place = [jax.random.randint(jax.random.fold_in(rng, axis), (), 0, length) for axis, length in enumerate(result.shape)]
    longest = result.shape.index(max(result.shape))
    beside = place[:longest] + [(place[longest] + 1) % result.shape[longest]] + place[longest + 1:]
    return result.at[tuple(place)].set(least).at[tuple(beside)].set(top_value)


def block_scale(key, dims, pieces, smallest, largest):
    gain = 1.0
    for dim, blocks in pieces:
        steps = jax.random.uniform(jax.random.fold_in(jax.random.fold_in(key, 6), dim), (blocks,), jnp.float32, smallest / len(pieces), largest / len(pieces))
        gain = gain * jnp.repeat(jnp.exp(steps), dims[dim] // blocks).reshape((-1,) + (1,) * (len(dims) - 1 - dim))
    return gain


def scatter_about(rng, dims, scale, reach, shards=(), held_as=jnp.bfloat16):
    factor_of = block_scale(rng, dims, shards, -0.22, 0.18) if shards else 1.0
    array = jax.random.normal(rng, dims, jnp.float32) * scale * factor_of
    return jnp.minimum(jnp.maximum(array, -reach), reach).astype(held_as)


def setup_inputs(seed: int = 0) -> dict:
    streams_of = jax.random.split(jax.random.key(seed), 9)
    features = scatter_about(streams_of[0], (NODES, D), 1.0, 6.0, ((0, 512),))
    neighbours = draw_neighbours(jax.random.fold_in(streams_of[8], 71), 0)
    send_rows = set_ends(jax.random.randint(streams_of[2], (SENDS, BLOCK), 0, NODE_DEV), jax.random.fold_in(streams_of[2], 1), 0, NODE_DEV - 1).astype(jnp.int32)
    block_counts = draw_block_counts(jax.random.fold_in(streams_of[8], 71), 0)
    hub_rows = set_ends(jax.random.randint(streams_of[4], (OWNERS, HUB_DEV), 0, NODE_DEV), jax.random.fold_in(streams_of[4], 1), 0, NODE_DEV - 1).astype(jnp.int32)
    w_self = scatter_about(streams_of[5], (D, D), D ** -0.5, 0.375)
    w_nbr = scatter_about(streams_of[6], (D, D), D ** -0.5, 0.375)
    cotangent = scatter_about(streams_of[7], (NODES, D), 1.0, 6.0, ((0, 512),))
    return dict(features=features, neighbours=neighbours, send_rows=send_rows, block_counts=block_counts, hub_rows=hub_rows, w_self=w_self, w_nbr=w_nbr, cotangent=cotangent)


def reference(features, neighbours, send_rows, block_counts, hub_rows, w_self, w_nbr, cotangent):
    node_total = features.shape[0]
    device = (jnp.arange(node_total, dtype=jnp.int32) // NODE_DEV)[:, None]
    group_id = device // N_MEMBER
    member_id = device % N_MEMBER
    local_id = device * NODE_DEV + jnp.clip(neighbours, 0, NODE_DEV - 1)
    shifted = jnp.clip(neighbours - NODE_DEV, 0, N_MEMBER * BLOCK - 1)
    peer = shifted // BLOCK
    slot = shifted % BLOCK
    sender = group_id * N_MEMBER + peer
    pair = sender * N_MEMBER + member_id
    sent = send_rows[pair, slot]
    valid = slot < block_counts[pair]
    border_id = jnp.where(valid, sender * NODE_DEV + sent, node_total)
    hub_pos = jnp.clip(neighbours - NODE_DEV - N_MEMBER * BLOCK, 0, N_GROUP * N_MEMBER * HUB_DEV - 1)
    owner = hub_pos // HUB_DEV
    hub_id = owner * NODE_DEV + hub_rows[owner, hub_pos % HUB_DEV]
    source = jnp.where(neighbours < NODE_DEV, local_id, jnp.where(neighbours < NODE_DEV + N_MEMBER * BLOCK, border_id, hub_id)).astype(jnp.int32)
    extended = jnp.concatenate([features, jnp.zeros((1, D), jnp.bfloat16)], axis=0)
    agg_sum = jnp.zeros((node_total, D), jnp.float32)
    for sample in range(FANOUT):
        agg_sum = agg_sum + extended[source[:, sample]].astype(jnp.float32)
    agg = (agg_sum / FANOUT).astype(jnp.bfloat16)
    pre = jnp.dot(features, w_self, preferred_element_type=jnp.float32) + jnp.dot(agg, w_nbr, preferred_element_type=jnp.float32)
    sigma = jax.nn.sigmoid(pre)
    dpre = (cotangent.astype(jnp.float32) * sigma * (1.0 + pre * (1.0 - sigma))).astype(jnp.bfloat16)
    scale = 1.0 / math.sqrt(node_total)
    grad_self = jnp.dot(features.T, dpre, preferred_element_type=jnp.float32) * scale
    grad_nbr = jnp.dot(agg.T, dpre, preferred_element_type=jnp.float32) * scale
    own_grad = jnp.dot(dpre, w_self.T, preferred_element_type=jnp.float32)
    dagg = jnp.dot(dpre, w_nbr.T, preferred_element_type=jnp.float32) / FANOUT
    spread = jnp.zeros((node_total + 1, D), jnp.float32)
    for sample in range(FANOUT):
        spread = spread.at[source[:, sample]].add(dagg)
    grad_features = (own_grad + spread[:node_total]).astype(jnp.bfloat16)
    return (grad_self, grad_nbr, grad_features)
```

```python
import math

import jax
import jax.numpy as jnp
from jax import lax
from jax.sharding import Mesh, PartitionSpec as P

BF = jnp.bfloat16
F32 = jnp.float32
GROUP = ("x", "core")
MEMBER = ("y", "z")
ALL = ("x", "core", "y", "z")


def swap_blocks(array, axes):
    return lax.all_to_all(array, axes, split_axis=0, concat_axis=0, tiled=True)


def local(features, neighbours, send_rows, block_counts, hub_rows, w_self, w_nbr, cotangent):
    nodes, width = features.shape
    members, slots = send_rows.shape
    fan = neighbours.shape[1]
    hubs = hub_rows.shape[1]
    groups = lax.axis_size(GROUP)
    xs = lax.axis_size("x")
    wide = 24
    scale = 1.0 / math.sqrt(nodes * groups * members)

    keep = jnp.arange(slots, dtype=jnp.int32)[None, :] < block_counts[:, None]
    sent = jnp.where(keep, send_rows, -1)
    row_ids = jnp.concatenate(
        [
            sent,
            jnp.broadcast_to(hub_rows, (members, hubs)),
            jnp.full((members, wide - slots - hubs), -1, jnp.int32),
        ],
        axis=1,
    ).reshape(members * wide, 1)
    node_iota = jnp.arange(nodes, dtype=jnp.int32)
    pick = (row_ids == node_iota[None, :]).astype(BF)
    outgoing = jnp.dot(pick, features, preferred_element_type=F32).astype(BF)
    incoming = swap_blocks(outgoing, MEMBER)
    my_hubs = incoming.reshape(members, wide, width)[:, slots : slots + hubs].reshape(members * hubs, width)
    hub_table = lax.all_gather(my_hubs, GROUP, axis=0, tiled=True)

    border = neighbours - nodes
    border_stop = members * slots
    column = jnp.where(
        border < 0,
        neighbours,
        jnp.where(
            border < border_stop,
            nodes + (border // slots) * wide + border % slots,
            border - border_stop + nodes + members * wide,
        ),
    )
    total = nodes + members * wide + groups * members * hubs
    ids = jnp.arange(total, dtype=jnp.int32)
    counts = jnp.zeros((nodes, total), BF)
    for f in range(fan):
        counts = counts + (column[:, f : f + 1] == ids[None, :]).astype(BF)
    first, second = nodes, nodes + members * wide
    agg_sum = (
        jnp.dot(counts[:, :first], features, preferred_element_type=F32)
        + jnp.dot(counts[:, first:second], incoming, preferred_element_type=F32)
        + jnp.dot(counts[:, second:], hub_table, preferred_element_type=F32)
    )
    agg = (agg_sum / fan).astype(BF)
    pre = jnp.dot(features, w_self, preferred_element_type=F32) + jnp.dot(agg, w_nbr, preferred_element_type=F32)
    sigma = jax.nn.sigmoid(pre)
    dpre = (cotangent.astype(F32) * sigma * (1.0 + pre * (1.0 - sigma))).astype(BF)

    over_rows = (((0,), (0,)), ((), ()))
    own_grad = jnp.dot(dpre, w_self.T, preferred_element_type=F32)
    dagg = (jnp.dot(dpre, w_nbr.T, preferred_element_type=F32) / fan).astype(BF)
    spread = lax.dot_general(counts, dagg, over_rows, preferred_element_type=F32)
    part = lax.dot_general(jnp.concatenate([features, agg], axis=1), dpre, over_rows, preferred_element_type=F32)

    border_grad = spread[first:second].astype(BF).reshape(members, wide, width)
    weight_rows = 2 * width // members
    outward = jnp.concatenate(
        [border_grad[:, :slots], part.astype(BF).reshape(members, weight_rows, width)], axis=1
    ).reshape(members * wide, width)
    returned = swap_blocks(outward, MEMBER).reshape(members, wide, width)
    weight_sum = jnp.sum(returned[:, slots:].astype(F32), axis=0).astype(BF)
    weight_all = swap_blocks(jnp.broadcast_to(weight_sum, (groups, weight_rows, width)).reshape(-1, width), GROUP)
    weight_done = jnp.sum(weight_all.reshape(groups, weight_rows, width).astype(F32), axis=0)

    hub_grad = spread[second:].astype(BF).reshape(xs, 2, members * hubs, width)
    core = lax.axis_index("core")
    mine = lax.dynamic_index_in_dim(hub_grad, core, 1, keepdims=False)
    other = lax.dynamic_index_in_dim(hub_grad, 1 - core, 1, keepdims=False)
    met = lax.ppermute(other, "core", [(0, 1), (1, 0)])
    paired = (mine.astype(F32) + met.astype(F32)).astype(BF)
    along = swap_blocks(paired.reshape(xs * members * hubs, width), "x")
    hub_part = jnp.sum(along.reshape(xs, members, hubs, width).astype(F32), axis=0).astype(BF)
    last = 16
    final = jnp.concatenate(
        [
            jnp.broadcast_to((weight_done * scale).astype(BF), (members, weight_rows, width)),
            hub_part,
            jnp.zeros((members, last - weight_rows - hubs, width), BF),
        ],
        axis=1,
    ).reshape(members * last, width)
    final = swap_blocks(final, MEMBER).reshape(members, last, width)
    weights = final[:, :weight_rows].reshape(2 * width, width).astype(F32)
    hub_mine = jnp.sum(final[:, weight_rows : weight_rows + hubs].astype(F32), axis=0)

    back = jnp.concatenate([returned[:, :slots].reshape(members * slots, width), hub_mine.astype(BF)], axis=0)
    home = jnp.concatenate([sent.reshape(1, -1), hub_rows], axis=1)
    place = (node_iota[:, None] == home).astype(BF)
    grad = own_grad + spread[:first] + jnp.dot(place, back, preferred_element_type=F32)
    return weights[:width], weights[width:], grad.astype(BF)


def solution(mesh):
    split = Mesh(mesh.devices.reshape(4, 2, 8, 8), ALL)
    rows = P(ALL, None)
    in_specs = (rows, rows, rows, P(ALL), rows, P(), P(), rows)
    out_specs = (P(), P(), rows)
    return jax.shard_map(local, mesh=split, in_specs=in_specs, out_specs=out_specs, check_vma=False)
```

```python
import functools
import math

import jax
import jax.numpy as jnp
from jax import lax
from jax.experimental import pallas as pl
from jax.experimental.pallas import tpu as pltpu
from jax.sharding import Mesh, PartitionSpec as P

BF = jnp.bfloat16
F32 = jnp.float32
I32 = jnp.int32
GROUP = ("x", "core")
MEMBER = ("y", "z")
ALL = ("x", "core", "y", "z")

D = 256
NODES = 256
FAN = 10
MEMBERS = 64
SLOTS = 16
HUBS = 4
GROUPS = 8
XS = 4
HALF = MEMBERS * 8
BORDER = NODES + 2 * HALF
SIDE = XS * MEMBERS * HUBS
TABLE = BORDER + 2 * SIDE
SCALE = 1.0 / math.sqrt(NODES * GROUPS * MEMBERS)
OVER_ROWS = (((0,), (0,)), ((), ()))
OVER_COLS = (((1,), (1,)), ((), ()))

VMEM = pl.BlockSpec(memory_space=pltpu.VMEM)
SMEM = pl.BlockSpec(memory_space=pltpu.SMEM)


def iota(shape, dim):
    return lax.broadcasted_iota(I32, shape, dim)


def dot(a, b):
    return jnp.dot(a, b, preferred_element_type=F32)


def call(body, name, outs, smem, flops, moved, *args):
    return pl.pallas_call(
        body,
        name=name,
        out_shape=[jax.ShapeDtypeStruct(s, t) for s, t in outs],
        in_specs=[SMEM] * smem + [VMEM] * (len(args) - smem),
        out_specs=[VMEM] * len(outs),
        compiler_params=pltpu.CompilerParams(vmem_limit_bytes=40 * 1024 * 1024),
        cost_estimate=pl.CostEstimate(flops=flops, bytes_accessed=moved, transcendentals=0),
    )(*args)


def split_rows(rows):
    left = rows[:, :128].reshape(-1, 8, 128)
    right = rows[:, 128:].reshape(-1, 8, 128)
    low = iota(left.shape, 1) < 4
    even = jnp.where(low, left, pltpu.roll(right, 4, 1))
    odd = jnp.where(low, pltpu.roll(left, 4, 1), right)
    return jnp.stack([even, odd], axis=1).reshape(-1, 8, 128)


def join_rows(tiles):
    pairs = tiles.reshape(-1, 2, 8, 128)
    even, odd = pairs[:, 0], pairs[:, 1]
    low = iota(even.shape, 1) < 4
    left = jnp.where(low, even, pltpu.roll(odd, 4, 1)).reshape(-1, 128)
    right = jnp.where(low, pltpu.roll(even, 4, 1), odd).reshape(-1, 128)
    return left, right


def outgoing_rows(hub, send, count, features, out, pick):
    member = iota((HALF, MEMBERS), 0) >> 3
    own = member == iota((HALF, MEMBERS), 1)
    spread = lax.dot_general(
        own.astype(F32).astype(BF), send[...].astype(F32).astype(BF), OVER_COLS, preferred_element_type=F32
    )
    live = jnp.sum(jnp.where(own, count[...].astype(F32), 0.0), axis=1, keepdims=True)
    lane = iota((HALF, SLOTS), 1)
    slot = iota((HALF, SLOTS), 0) & 7
    place = (iota((HALF, 1), 0) & 7).astype(F32)
    nodes = iota((HALF, NODES), 1).astype(F32)
    f = features[...]
    for a in range(2):
        row = jnp.sum(jnp.where(lane == slot + 8 * a, spread, 0.0), axis=1, keepdims=True)
        row = jnp.where(place + 8.0 * a < live, row, -1.0)
        hot = (nodes == row).astype(F32).astype(BF)
        pick[a * HALF : (a + 1) * HALF, :] = hot
        out[:, a * D : (a + 1) * D] = dot(hot, f).astype(BF)
    which = iota((16, NODES), 0) & 3
    ids = jnp.full((16, NODES), hub[0, 0], I32)
    for h in range(1, HUBS):
        ids = jnp.where(which == h, hub[0, h], ids)
    rows = dot((ids == iota((16, NODES), 1)).astype(F32).astype(BF), f)
    tile = jnp.where(iota((8, 128), 0) < 4, rows[:8, :128], rows[:8, 128:])
    out[:, 2 * D :] = jnp.broadcast_to(tile[None], (MEMBERS, 8, 128)).reshape(HALF, 128).astype(BF)


def table_row(n, core):
    b = n - NODES
    h = b - MEMBERS * SLOTS
    border = NODES + ((b >> 3) & 1) * HALF + (b >> 4) * 8 + (b & 7)
    side = ((h >> 8) & 1) ^ core
    hub = BORDER + side * SIDE + (h >> 9) * 256 + (h & 255)
    return jnp.where(b < 0, n, jnp.where(h < 0, border, hub))


def count_rows(core, near_t, pick, features, w_self, counts, counts_t, home, pre_self):
    row_t = table_row(near_t[...], core[0])
    step = 32

    @pl.loop(0, TABLE // step)
    def _(i):
        base = pl.multiple_of(i * step, step)
        ids = iota((step, NODES), 0) + base
        total = jnp.zeros((step, NODES), F32)
        for f in range(FAN):
            total = total + jnp.where(ids == row_t[f : f + 1, :], 1.0, 0.0)
        counts_t[pl.ds(base, step), :] = total.astype(BF)

    eye = (iota((NODES, NODES), 0) == iota((NODES, NODES), 1)).astype(F32).astype(BF)
    for t in range(TABLE // 256):
        block = lax.dot_general(eye, counts_t[t * 256 : (t + 1) * 256, :], OVER_COLS, preferred_element_type=F32)
        counts[:, t * 256 : (t + 1) * 256] = block.astype(BF)
    home[...] = lax.dot_general(eye, pick[...], OVER_COLS, preferred_element_type=F32).astype(BF)
    pre_self[...] = dot(features[...], w_self[...])


def own_hubs(incoming, out):
    left, right = join_rows(incoming[:, 2 * D :].astype(F32).reshape(MEMBERS, 8, 128))
    left, right = left.astype(BF), right.astype(BF)
    for x in range(XS):
        out[x * 256 : (x + 1) * 256, :128] = left
        out[x * 256 : (x + 1) * 256, 128:] = right


def forward(counts, counts_t, features, incoming, mine, other, pre_self, w_nbr, cotangent, outward, dagg_out, dpre_out):
    f = features[...]
    total = dot(counts[:, :NODES], f)
    total += dot(counts[:, NODES : NODES + HALF], incoming[:, :D])
    total += dot(counts[:, NODES + HALF : BORDER], incoming[:, D : 2 * D])
    total += dot(counts[:, BORDER : BORDER + SIDE], mine[...])
    total += dot(counts[:, BORDER + SIDE :], other[...])
    agg = (total / FAN).astype(BF)
    pre = pre_self[...] + dot(agg, w_nbr[...])
    sigma = 1.0 / (1.0 + jnp.exp(-pre))
    dpre = (cotangent[...].astype(F32) * sigma * (1.0 + pre * (1.0 - sigma))).astype(BF)
    dagg = (lax.dot_general(dpre, w_nbr[...], OVER_COLS, preferred_element_type=F32) / FAN).astype(BF)
    dpre_out[...] = dpre
    dagg_out[...] = dagg
    outward[:, :D] = dot(counts_t[NODES : NODES + HALF, :], dagg).astype(BF)
    outward[:, D : 2 * D] = dot(counts_t[NODES + HALF : BORDER, :], dagg).astype(BF)
    outward[:D, 2 * D :] = lax.dot_general(f, dpre, OVER_ROWS, preferred_element_type=F32).astype(BF)
    outward[D:, 2 * D :] = lax.dot_general(agg, dpre, OVER_ROWS, preferred_element_type=F32).astype(BF)


def other_hubs(counts_t, dagg, out):
    out[...] = dot(counts_t[BORDER + SIDE :, :], dagg[...]).astype(BF)


def mine_and_own(counts_t, dagg, dpre, w_self, hubs, own):
    hubs[...] = dot(counts_t[BORDER : BORDER + SIDE, :], dagg[...]).astype(BF)
    own[...] = dot(counts_t[:NODES, :], dagg[...]) + lax.dot_general(
        dpre[...], w_self[...], OVER_COLS, preferred_element_type=F32
    )


def pair_hubs(x, hubs, met, kept, *to):
    for k, out in enumerate((kept,) + to):
        place = lax.rem(x[0] + k, XS)
        rows = pl.ds(pl.multiple_of(place * 256, 256), 256)
        out[...] = (hubs[rows, :].astype(F32) + met[rows, :].astype(F32)).astype(BF)


def sum_hubs(kept, a, b, c, out):
    total = kept[...].astype(F32) + a[...].astype(F32) + b[...].astype(F32) + c[...].astype(F32)
    out[...] = split_rows(total).reshape(HALF, 128).astype(BF)


def sum_weights(returned, out):
    total = jnp.sum(returned[:, 2 * D :].astype(F32).reshape(MEMBERS, 8, D), axis=0)
    out[...] = jnp.broadcast_to(total[None], (GROUPS, 8, D)).reshape(GROUPS * 8, D).astype(BF)


def add_returned(returned, home, own, out):
    total = own[...] + dot(home[:, :HALF], returned[:, :D])
    out[...] = total + dot(home[:, HALF:], returned[:, D : 2 * D])


def last_message(weights, hubs, out):
    total = jnp.sum(weights[...].astype(F32).reshape(GROUPS, 8, D), axis=0) * SCALE
    out[:, :D] = jnp.broadcast_to(total[None], (MEMBERS, 8, D)).reshape(HALF, D).astype(BF)
    out[:, D:] = hubs[...]


def finish(hub, last, partial, grad_self, grad_nbr, grad):
    grad_self[...] = last[:D, :D].astype(F32)
    grad_nbr[...] = last[D:, :D].astype(F32)
    tile = jnp.sum(last[:, D:].astype(F32).reshape(MEMBERS, 8, 128), axis=0)
    total = partial[...]
    node = iota((NODES, D), 0)
    for h in range(HUBS):
        row = jnp.concatenate([tile[h : h + 1], tile[h + 4 : h + 5]], axis=1)
        total = total + jnp.where(node == hub[0, h], row, 0.0)
    grad[...] = total.astype(BF)


def exchange(array, axes, parts):
    block = array.reshape(parts, -1, array.shape[1])
    return lax.all_to_all(block, axes, split_axis=0, concat_axis=0, tiled=True).reshape(array.shape)


def local(features, neighbours, send_rows, block_counts, hub_rows, w_self, w_nbr, cotangent):
    core = lax.axis_index("core").reshape(1)
    x = lax.axis_index("x").reshape(1)
    counts_in = block_counts.reshape(1, MEMBERS)
    outgoing, pick = call(
        outgoing_rows, "outgoing_rows", [((HALF, 640), BF), ((2 * HALF, NODES), BF)], 1, 2**27, 2**20,
        hub_rows, send_rows.T, counts_in, features,
    )
    incoming = exchange(outgoing, MEMBER, MEMBERS)
    counts, counts_t, home, pre_self = call(
        count_rows, "count_rows",
        [((NODES, TABLE), BF), ((TABLE, NODES), BF), ((NODES, 2 * HALF), BF), ((NODES, D), F32)],
        1, 2**30, 2**22,
        core, neighbours.T, pick, features, w_self,
    )
    (mine,) = call(own_hubs, "own_hubs", [((SIDE, D), BF)], 0, 2**16, 2**19, incoming)
    mine = exchange(mine, "x", XS)
    swap = [(0, 1), (1, 0)]
    other = lax.ppermute(mine, "core", swap)
    outward, dagg, dpre = call(
        forward, "forward", [((HALF, 768), BF), ((NODES, D), BF), ((NODES, D), BF)], 0, 2**30, 2**23,
        counts, counts_t, features, incoming, mine, other, pre_self, w_nbr, cotangent,
    )
    returned = exchange(outward, MEMBER, MEMBERS)

    (theirs,) = call(other_hubs, "other_hubs", [((SIDE, D), BF)], 0, 2**27, 2**20, counts_t, dagg)
    met = lax.ppermute(theirs, "core", swap)
    hubs, own = call(
        mine_and_own, "mine_and_own", [((SIDE, D), BF), ((NODES, D), F32)], 0, 2**28, 2**21, counts_t, dagg, dpre, w_self
    )
    block = ((NODES, D), BF)
    kept, *to = call(pair_hubs, "pair_hubs", [block] * XS, 1, 2**18, 2**20, x, hubs, met)
    came = [lax.ppermute(to[k - 1], "x", [(i, (i + k) % XS) for i in range(XS)]) for k in range(1, XS)]
    (hub_tiles,) = call(sum_hubs, "sum_hubs", [((HALF, 128), BF)], 0, 2**18, 2**20, kept, *came)

    (weights,) = call(sum_weights, "sum_weights", [((GROUPS * 8, D), BF)], 0, 2**17, 2**18, returned)
    weights = exchange(weights, GROUP, GROUPS)
    (partial,) = call(add_returned, "add_returned", [((NODES, D), F32)], 0, 2**27, 2**20, returned, home, own)
    (message,) = call(last_message, "last_message", [((HALF, 384), BF)], 0, 2**17, 2**18, weights, hub_tiles)
    last = exchange(message, MEMBER, MEMBERS)
    return tuple(
        call(
            finish, "finish", [((D, D), F32), ((D, D), F32), ((NODES, D), BF)], 1, 2**18, 2**20, hub_rows, last, partial
        )
    )


def solution(mesh):
    split = Mesh(mesh.devices.reshape(XS, 2, 8, 8), ALL)
    rows = P(ALL, None)
    in_specs = (rows, rows, rows, P(ALL), rows, P(), P(), rows)
    out_specs = (P(), P(), rows)
    return jax.shard_map(local, mesh=split, in_specs=in_specs, out_specs=out_specs, check_vma=False)
```

```python
import math

import jax
import jax.numpy as jnp
from jax import lax
from jax.experimental import pallas as pl
from jax.experimental.pallas import tpu as pltpu
from jax.sharding import Mesh, PartitionSpec as P

BF = jnp.bfloat16
F32 = jnp.float32
I32 = jnp.int32
GROUP = ("x", "core")
MEMBER = ("y", "z")
ALL = ("x", "core", "y", "z")

D = 256
NODES = 256
FAN = 10
MEMBERS = 64
SLOTS = 16
HUBS = 4
GROUPS = 8
XS = 4
HALF = MEMBERS * 8
BORDER = NODES + 2 * HALF
SIDE = XS * MEMBERS * HUBS
TABLE = BORDER + 2 * SIDE
SCALE = 1.0 / math.sqrt(NODES * GROUPS * MEMBERS)
OVER_ROWS = (((0,), (0,)), ((), ()))
OVER_COLS = (((1,), (1,)), ((), ()))

VMEM = pl.BlockSpec(memory_space=pltpu.VMEM)
SMEM = pl.BlockSpec(memory_space=pltpu.SMEM)
HBM = pl.BlockSpec(memory_space=pltpu.HBM)
ANY = pl.BlockSpec(memory_space=pl.ANY)


def iota(shape, dim):
    return lax.broadcasted_iota(I32, shape, dim)


def dot(a, b):
    return jnp.dot(a, b, preferred_element_type=F32)


def call(body, name, outs, flops, moved, *args, kept=(), smem=(), unread=(), to_hbm=(), scratch=()):
    places = [HBM if i in kept else SMEM if i in smem else ANY if i in unread else VMEM for i in range(len(args))]
    return pl.pallas_call(
        body,
        name=name,
        out_shape=[(pltpu.HBM if i in to_hbm else jax.ShapeDtypeStruct)(s, t) for i, (s, t) in enumerate(outs)],
        in_specs=places,
        out_specs=[HBM if i in to_hbm else VMEM for i in range(len(outs))],
        scratch_shapes=list(scratch),
        compiler_params=pltpu.CompilerParams(vmem_limit_bytes=40 * 1024 * 1024),
        cost_estimate=pl.CostEstimate(flops=flops, bytes_accessed=moved, transcendentals=0),
    )(*[pltpu.with_memory_space_constraint(a, pltpu.HBM) if i in kept else a for i, a in enumerate(args)])


def send(sources, targets, sems, first=0):
    copies = [pltpu.make_async_copy(a, b, sems.at[first + i]) for i, (a, b) in enumerate(zip(sources, targets))]
    for copy in copies:
        copy.start()
    return copies


def finished(copies):
    for copy in copies:
        copy.wait()


def split_rows(rows):
    left = rows[:, :128].reshape(-1, 8, 128)
    right = rows[:, 128:].reshape(-1, 8, 128)
    low = iota(left.shape, 1) < 4
    even = jnp.where(low, left, pltpu.roll(right, 4, 1))
    odd = jnp.where(low, pltpu.roll(left, 4, 1), right)
    return jnp.stack([even, odd], axis=1).reshape(-1, 8, 128)


def join_rows(tiles):
    pairs = tiles.reshape(-1, 2, 8, 128)
    even, odd = pairs[:, 0], pairs[:, 1]
    low = iota(even.shape, 1) < 4
    left = jnp.where(low, even, pltpu.roll(odd, 4, 1)).reshape(-1, 128)
    right = jnp.where(low, pltpu.roll(even, 4, 1), odd).reshape(-1, 128)
    return left, right


def hot_rows(send_t, count):
    own = (iota((HALF, MEMBERS), 0) >> 3) == iota((HALF, MEMBERS), 1)
    spread = lax.dot_general(
        own.astype(F32).astype(BF), send_t.astype(F32).astype(BF), OVER_COLS, preferred_element_type=F32
    )
    live = jnp.sum(jnp.where(own, count.astype(F32), 0.0), axis=1, keepdims=True)
    lane = iota((HALF, SLOTS), 1)
    slot = iota((HALF, SLOTS), 0) & 7
    place = (iota((HALF, 1), 0) & 7).astype(F32)
    nodes = iota((HALF, NODES), 1).astype(F32)
    hot = []
    for a in range(2):
        row = jnp.sum(jnp.where(lane == slot + 8 * a, spread, 0.0), axis=1, keepdims=True)
        row = jnp.where(place + 8.0 * a < live, row, -1.0)
        hot.append((nodes == row).astype(F32).astype(BF))
    return hot


def hub_ids(hub, shape, h):
    return jnp.broadcast_to(jnp.sum(jnp.where(iota(hub.shape, 1) == h, hub, 0), axis=1, keepdims=True), shape)


def outgoing_rows(hub, send_t, count, features, out, hub_v, send_v, count_v, f_v, out_v, sems):
    copies = send((hub, send_t, count, features), (hub_v, send_v, count_v, f_v), sems)
    finished(copies)
    f = f_v[...]
    which = iota((16, NODES), 0) & 3
    ids = jnp.full((16, NODES), -1, I32)
    for h in range(HUBS):
        ids = jnp.where(which == h, hub_ids(hub_v[...], ids.shape, h), ids)
    rows = dot((ids == iota((16, NODES), 1)).astype(F32).astype(BF), f)
    tile = jnp.where(iota((8, 128), 0) < 4, rows[:8, :128], rows[:8, 128:])
    out_v[:, 2 * D :] = jnp.broadcast_to(tile[None], (MEMBERS, 8, 128)).reshape(HALF, 128).astype(BF)
    lanes = [slice(2 * D, 2 * D + 128), slice(0, D), slice(D, 2 * D)]
    copies = send([out_v.at[:, lanes[0]]], [out.at[:, lanes[0]]], sems, 4)
    for a, hot in enumerate(hot_rows(send_v[...], count_v[...])):
        out_v[:, lanes[a + 1]] = dot(hot, f).astype(BF)
        copies += send([out_v.at[:, lanes[a + 1]]], [out.at[:, lanes[a + 1]]], sems, 5 + a)
    finished(copies)


def table_row(n, core):
    b = n - NODES
    h = b - MEMBERS * SLOTS
    border = NODES + ((b >> 3) & 1) * HALF + (b >> 4) * 8 + (b & 7)
    side = ((h >> 8) & 1) ^ core
    hub = BORDER + side * SIDE + (h >> 9) * 256 + (h & 255)
    return jnp.where(b < 0, n, jnp.where(h < 0, border, hub))


def count_rows(core, near_t, send_t, count, features, w_self, after, counts, counts_t, home, pre_self):
    row_t = table_row(near_t[...], core[0])
    step = 32

    @pl.loop(0, TABLE // step)
    def _(i):
        base = pl.multiple_of(i * step, step)
        ids = iota((step, NODES), 0) + base
        total = jnp.zeros((step, NODES), F32)
        for f in range(FAN):
            total = total + jnp.where(ids == row_t[f : f + 1, :], 1.0, 0.0)
        counts_t[pl.ds(base, step), :] = total.astype(BF)

    eye = (iota((NODES, NODES), 0) == iota((NODES, NODES), 1)).astype(F32).astype(BF)
    for t in range(TABLE // 256):
        block = lax.dot_general(eye, counts_t[t * 256 : (t + 1) * 256, :], OVER_COLS, preferred_element_type=F32)
        counts[:, t * 256 : (t + 1) * 256] = block.astype(BF)
    for a, hot in enumerate(hot_rows(send_t[...], count[...])):
        block = lax.dot_general(eye, hot, OVER_COLS, preferred_element_type=F32)
        home[:, a * HALF : (a + 1) * HALF] = block.astype(BF)
    pre_self[...] = dot(features[...], w_self[...])


def own_hubs(incoming, after, out):
    left, right = join_rows(incoming[:, 2 * D :].astype(F32).reshape(MEMBERS, 8, 128))
    left, right = left.astype(BF), right.astype(BF)
    for x in range(XS):
        out[x * 256 : (x + 1) * 256, :128] = left
        out[x * 256 : (x + 1) * 256, 128:] = right


def forward(
    counts, counts_t, features, incoming, mine, other, pre_self, w_nbr, cotangent, w_self,
    outward, theirs, hubs, own, out_v, theirs_v, hubs_v, own_v, sems,
):
    f = features[...]
    total = dot(counts[:, :NODES], f)
    total += dot(counts[:, NODES : NODES + HALF], incoming[:, :D])
    total += dot(counts[:, NODES + HALF : BORDER], incoming[:, D : 2 * D])
    total += dot(counts[:, BORDER : BORDER + SIDE], mine[...])
    total += dot(counts[:, BORDER + SIDE :], other[...])
    agg = (total / FAN).astype(BF)
    pre = pre_self[...] + dot(agg, w_nbr[...])
    sigma = 1.0 / (1.0 + jnp.exp(-pre))
    dpre = (cotangent[...].astype(F32) * sigma * (1.0 + pre * (1.0 - sigma))).astype(BF)
    dagg = (lax.dot_general(dpre, w_nbr[...], OVER_COLS, preferred_element_type=F32) / FAN).astype(BF)

    out_v[:, :D] = dot(counts_t[NODES : NODES + HALF, :], dagg).astype(BF)
    out_v[:, D : 2 * D] = dot(counts_t[NODES + HALF : BORDER, :], dagg).astype(BF)
    copies = send([out_v.at[:, : 2 * D]], [outward.at[:, : 2 * D]], sems)
    out_v[:D, 2 * D :] = lax.dot_general(f, dpre, OVER_ROWS, preferred_element_type=F32).astype(BF)
    out_v[D:, 2 * D :] = lax.dot_general(agg, dpre, OVER_ROWS, preferred_element_type=F32).astype(BF)
    copies += send([out_v.at[:, 2 * D :]], [outward.at[:, 2 * D :]], sems, 1)
    theirs_v[...] = dot(counts_t[BORDER + SIDE :, :], dagg).astype(BF)
    copies += send([theirs_v], [theirs], sems, 2)
    hubs_v[...] = dot(counts_t[BORDER : BORDER + SIDE, :], dagg).astype(BF)
    own_v[...] = dot(counts_t[:NODES, :], dagg) + lax.dot_general(
        dpre, w_self[...], OVER_COLS, preferred_element_type=F32
    )
    copies += send([hubs_v, own_v], [hubs, own], sems, 3)
    finished(copies)


def pair_hubs(x, hubs, met, kept, *to):
    for k, out in enumerate((kept,) + to):
        place = lax.rem(x[0] + k, XS)
        rows = pl.ds(pl.multiple_of(place * 256, 256), 256)
        out[...] = (hubs[rows, :].astype(F32) + met[rows, :].astype(F32)).astype(BF)


def sum_hubs(kept, a, b, c, out):
    total = kept[...].astype(F32) + a[...].astype(F32) + b[...].astype(F32) + c[...].astype(F32)
    out[...] = split_rows(total).reshape(HALF, 128).astype(BF)


def sum_weights(returned, out):
    total = jnp.sum(returned[:, 2 * D :].astype(F32).reshape(MEMBERS, 8, D), axis=0)
    out[...] = jnp.broadcast_to(total[None], (GROUPS, 8, D)).reshape(GROUPS * 8, D).astype(BF)


def add_returned(returned, home, own, out):
    total = own[...] + dot(home[:, :HALF], returned[:, :D])
    out[...] = total + dot(home[:, HALF:], returned[:, D : 2 * D])


def last_message(weights, hubs, out):
    total = jnp.sum(weights[...].astype(F32).reshape(GROUPS, 8, D), axis=0) * SCALE
    out[:, :D] = jnp.broadcast_to(total[None], (MEMBERS, 8, D)).reshape(HALF, D).astype(BF)
    out[:, D:] = hubs[...]


def finish(hub, last, partial, grad_self, grad_nbr, grad, weights_v, grad_v, sems):
    weights_v[...] = last[:, :D].astype(F32)
    copies = send([weights_v.at[:D, :], weights_v.at[D:, :]], [grad_self, grad_nbr], sems)
    tile = jnp.sum(last[:, D:].astype(F32).reshape(MEMBERS, 8, 128), axis=0)
    total = partial[...]
    node = iota((NODES, D), 0)
    for h in range(HUBS):
        row = jnp.concatenate([tile[h : h + 1], tile[h + 4 : h + 5]], axis=1)
        total = total + jnp.where(node == hub_ids(hub[...], (NODES, D), h), row, 0.0)
    grad_v[...] = total.astype(BF)
    copies += send([grad_v], [grad], sems, 2)
    finished(copies)


def exchange(array, axes, parts):
    block = array.reshape(parts, -1, array.shape[1])
    return lax.all_to_all(block, axes, split_axis=0, concat_axis=0, tiled=True).reshape(array.shape)


def local(features, neighbours, send_rows, block_counts, hub_rows, w_self, w_nbr, cotangent):
    core = lax.axis_index("core").reshape(1)
    x = lax.axis_index("x").reshape(1)
    send_t = send_rows.T
    live = block_counts.reshape(1, MEMBERS)
    side = ((SIDE, D), BF)
    (outgoing,) = call(
        outgoing_rows, "outgoing_rows", [((HALF, 640), BF)], 2**27, 2**20,
        hub_rows, send_t, live, features,
        kept=range(4), to_hbm=(0,),
        scratch=[
            pltpu.VMEM((1, HUBS), I32), pltpu.VMEM((SLOTS, MEMBERS), I32), pltpu.VMEM((1, MEMBERS), I32),
            pltpu.VMEM((NODES, D), BF), pltpu.VMEM((HALF, 640), BF), pltpu.SemaphoreType.DMA((7,)),
        ],
    )
    incoming = exchange(outgoing, MEMBER, MEMBERS)
    counts, counts_t, home, pre_self = call(
        count_rows, "count_rows",
        [((NODES, TABLE), BF), ((TABLE, NODES), BF), ((NODES, 2 * HALF), BF), ((NODES, D), F32)], 2**30, 2**22,
        core, neighbours.T, send_t, live, features, w_self, outgoing,
        smem=(0,), unread=(6,),
    )
    (mine,) = call(own_hubs, "own_hubs", [side], 2**16, 2**19, incoming, pre_self, unread=(1,))
    mine = exchange(mine, "x", XS)
    swap = [(0, 1), (1, 0)]
    other = lax.ppermute(mine, "core", swap)
    outward, theirs, hubs, own = call(
        forward, "forward", [((HALF, 768), BF), side, side, ((NODES, D), F32)], 2**30, 2**23,
        counts, counts_t, features, incoming, mine, other, pre_self, w_nbr, cotangent, w_self,
        to_hbm=range(4),
        scratch=[
            pltpu.VMEM((HALF, 768), BF), pltpu.VMEM((SIDE, D), BF), pltpu.VMEM((SIDE, D), BF),
            pltpu.VMEM((NODES, D), F32), pltpu.SemaphoreType.DMA((5,)),
        ],
    )
    returned = exchange(outward, MEMBER, MEMBERS)

    met = lax.ppermute(theirs, "core", swap)
    block = ((NODES, D), BF)
    kept, *to = call(pair_hubs, "pair_hubs", [block] * XS, 2**18, 2**20, x, hubs, met, smem=(0,))
    came = [lax.ppermute(to[k - 1], "x", [(i, (i + k) % XS) for i in range(XS)]) for k in range(1, XS)]
    (hub_tiles,) = call(sum_hubs, "sum_hubs", [((HALF, 128), BF)], 2**18, 2**20, kept, *came)

    (weights,) = call(sum_weights, "sum_weights", [((GROUPS * 8, D), BF)], 2**17, 2**18, returned)
    weights = exchange(weights, GROUP, GROUPS)
    (partial,) = call(add_returned, "add_returned", [((NODES, D), F32)], 2**27, 2**20, returned, home, own)
    (message,) = call(last_message, "last_message", [((HALF, 384), BF)], 2**17, 2**18, weights, hub_tiles)
    last = exchange(message, MEMBER, MEMBERS)
    return tuple(
        call(
            finish, "finish", [((D, D), F32), ((D, D), F32), ((NODES, D), BF)], 2**18, 2**20, hub_rows, last, partial,
            to_hbm=range(3),
            scratch=[pltpu.VMEM((2 * D, D), F32), pltpu.VMEM((NODES, D), BF), pltpu.SemaphoreType.DMA((3,))],
        )
    )


def solution(mesh):
    split = Mesh(mesh.devices.reshape(XS, 2, 8, 8), ALL)
    rows = P(ALL, None)
    in_specs = (rows, rows, rows, P(ALL), rows, P(), P(), rows)
    out_specs = (P(), P(), rows)
    return jax.shard_map(local, mesh=split, in_specs=in_specs, out_specs=out_specs, check_vma=False)
```

```python
import math

import jax
import jax.numpy as jnp
from jax import lax
from jax.experimental import pallas as pl
from jax.experimental.pallas import tpu as pltpu
from jax.sharding import Mesh, PartitionSpec as P

BF = jnp.bfloat16
F32 = jnp.float32
I32 = jnp.int32
GROUP = ("x", "core")
MEMBER = ("y", "z")
ALL = ("x", "core", "y", "z")

D = 256
NODES = 256
FAN = 10
MEMBERS = 64
SLOTS = 16
HUBS = 4
GROUPS = 8
XS = 4
HALF = MEMBERS * 8
BORDER = NODES + 2 * HALF
SIDE = XS * MEMBERS * HUBS
TABLE = BORDER + 2 * SIDE
SCALE = 1.0 / math.sqrt(NODES * GROUPS * MEMBERS)
OVER_ROWS = (((0,), (0,)), ((), ()))
OVER_COLS = (((1,), (1,)), ((), ()))

VMEM = pl.BlockSpec(memory_space=pltpu.VMEM)
SMEM = pl.BlockSpec(memory_space=pltpu.SMEM)
HBM = pl.BlockSpec(memory_space=pltpu.HBM)
ANY = pl.BlockSpec(memory_space=pl.ANY)


def iota(shape, dim):
    return lax.broadcasted_iota(I32, shape, dim)


def dot(a, b):
    return jnp.dot(a, b, preferred_element_type=F32)


def call(body, name, outs, flops, moved, *args, kept=(), smem=(), unread=(), to_hbm=(), scratch=(), alias={}):
    places = [HBM if i in kept else SMEM if i in smem else ANY if i in unread else VMEM for i in range(len(args))]
    return pl.pallas_call(
        body,
        name=name,
        out_shape=[(pltpu.HBM if i in to_hbm else jax.ShapeDtypeStruct)(s, t) for i, (s, t) in enumerate(outs)],
        in_specs=places,
        out_specs=[HBM if i in to_hbm else VMEM for i in range(len(outs))],
        scratch_shapes=list(scratch),
        input_output_aliases=alias,
        compiler_params=pltpu.CompilerParams(vmem_limit_bytes=16 * 1024 * 1024),
        cost_estimate=pl.CostEstimate(flops=flops, bytes_accessed=moved, transcendentals=0),
    )(*[pltpu.with_memory_space_constraint(a, pltpu.HBM) if i in kept else a for i, a in enumerate(args)])


def send(sources, targets, sems, first=0):
    copies = [pltpu.make_async_copy(a, b, sems.at[first + i]) for i, (a, b) in enumerate(zip(sources, targets))]
    for copy in copies:
        copy.start()
    return copies


def finished(copies):
    for copy in copies:
        copy.wait()


def split_rows(rows):
    left = rows[:, :128].reshape(-1, 8, 128)
    right = rows[:, 128:].reshape(-1, 8, 128)
    low = iota(left.shape, 1) < 4
    even = jnp.where(low, left, pltpu.roll(right, 4, 1))
    odd = jnp.where(low, pltpu.roll(left, 4, 1), right)
    return jnp.stack([even, odd], axis=1).reshape(-1, 8, 128)


def join_rows(tiles):
    pairs = tiles.reshape(-1, 2, 8, 128)
    even, odd = pairs[:, 0], pairs[:, 1]
    low = iota(even.shape, 1) < 4
    left = jnp.where(low, even, pltpu.roll(odd, 4, 1)).reshape(-1, 128)
    right = jnp.where(low, pltpu.roll(even, 4, 1), odd).reshape(-1, 128)
    return left, right


def hot_rows(send_t, count):
    own = (iota((HALF, MEMBERS), 0) >> 3) == iota((HALF, MEMBERS), 1)
    spread = lax.dot_general(
        own.astype(F32).astype(BF), send_t.astype(F32).astype(BF), OVER_COLS, preferred_element_type=F32
    )
    live = jnp.sum(jnp.where(own, count.astype(F32), 0.0), axis=1, keepdims=True)
    lane = iota((HALF, SLOTS), 1)
    slot = iota((HALF, SLOTS), 0) & 7
    place = (iota((HALF, 1), 0) & 7).astype(F32)
    nodes = iota((HALF, NODES), 1).astype(F32)
    hot = []
    for a in range(2):
        row = jnp.sum(jnp.where(lane == slot + 8 * a, spread, 0.0), axis=1, keepdims=True)
        row = jnp.where(place + 8.0 * a < live, row, -1.0)
        hot.append((nodes == row).astype(F32).astype(BF))
    return hot


def hub_ids(hub, shape, h):
    return jnp.broadcast_to(jnp.sum(jnp.where(iota(hub.shape, 1) == h, hub, 0), axis=1, keepdims=True), shape)


def outgoing_rows(hub, send_t, count, features, out, hub_v, send_v, count_v, f_v, out_v, sems):
    copies = send((send_t, count, hub, features), (send_v, count_v, hub_v, f_v), sems)
    finished(copies[:2])
    hot = hot_rows(send_v[...], count_v[...])
    finished(copies[2:])
    f = f_v[...]
    which = iota((16, NODES), 0) & 3
    ids = jnp.full((16, NODES), -1, I32)
    for h in range(HUBS):
        ids = jnp.where(which == h, hub_ids(hub_v[...], ids.shape, h), ids)
    rows = dot((ids == iota((16, NODES), 1)).astype(F32).astype(BF), f)
    tile = jnp.where(iota((8, 128), 0) < 4, rows[:8, :128], rows[:8, 128:])
    out_v[:, 2 * D :] = jnp.broadcast_to(tile[None], (MEMBERS, 8, 128)).reshape(HALF, 128).astype(BF)
    copies = send([out_v.at[:, 2 * D :]], [out.at[:, 2 * D :]], sems, 4)
    for a in range(2):
        lanes = slice(a * D, (a + 1) * D)
        out_v[:, lanes] = dot(hot[a], f).astype(BF)
        copies += send([out_v.at[:, lanes]], [out.at[:, lanes]], sems, 5 + a)
    finished(copies)


def table_row(n, core):
    b = n - NODES
    h = b - MEMBERS * SLOTS
    border = NODES + ((b >> 3) & 1) * HALF + (b >> 4) * 8 + (b & 7)
    side = ((h >> 8) & 1) ^ core
    hub = BORDER + side * SIDE + (h >> 9) * 256 + (h & 255)
    return jnp.where(b < 0, n, jnp.where(h < 0, border, hub))


def count_rows(core, near_t, send_t, count, features, w_self, after, counts, counts_t, home, pre_self, done):
    row_t = table_row(near_t[...], core[0])
    step = 32

    @pl.loop(0, TABLE // step)
    def _(i):
        base = pl.multiple_of(i * step, step)
        ids = iota((step, NODES), 0) + base
        total = jnp.zeros((step, NODES), F32)
        for f in range(FAN):
            total = total + jnp.where(ids == row_t[f : f + 1, :], 1.0, 0.0)
        counts_t[pl.ds(base, step), :] = total.astype(BF)

    eye = (iota((NODES, NODES), 0) == iota((NODES, NODES), 1)).astype(F32).astype(BF)
    for t in range(TABLE // 256):
        block = lax.dot_general(eye, counts_t[t * 256 : (t + 1) * 256, :], OVER_COLS, preferred_element_type=F32)
        counts[:, t * 256 : (t + 1) * 256] = block.astype(BF)
    for a, hot in enumerate(hot_rows(send_t[...], count[...])):
        block = lax.dot_general(eye, hot, OVER_COLS, preferred_element_type=F32)
        home[:, a * HALF : (a + 1) * HALF] = block.astype(BF)
    pre_self[...] = dot(features[...], w_self[...])
    done[...] = jnp.zeros((8, 128), F32)


def own_hubs(incoming, after, out, tiles, sems):
    finished(send([incoming.at[:, 2 * D :]], [tiles], sems))
    left, right = join_rows(tiles[...].astype(F32).reshape(MEMBERS, 8, 128))
    left, right = left.astype(BF), right.astype(BF)
    for x in range(XS):
        out[x * 256 : (x + 1) * 256, :128] = left
        out[x * 256 : (x + 1) * 256, 128:] = right


def near_sum(counts, features, incoming, mine, out):
    total = dot(counts[:, :NODES], features[...])
    total += dot(counts[:, NODES : NODES + HALF], incoming[:, :D])
    total += dot(counts[:, NODES + HALF : BORDER], incoming[:, D : 2 * D])
    out[...] = total + dot(counts[:, BORDER : BORDER + SIDE], mine[...])


def forward(
    counts, counts_t, features, near, other, pre_self, w_nbr, cotangent, outward, both, out_v, both_v, sems
):
    total = near[...] + dot(counts[:, BORDER + SIDE :], other[...])
    agg = (total / FAN).astype(BF)
    pre = pre_self[...] + dot(agg, w_nbr[...])
    sigma = 1.0 / (1.0 + jnp.exp(-pre))
    dpre = (cotangent[...].astype(F32) * sigma * (1.0 + pre * (1.0 - sigma))).astype(BF)
    dagg = (lax.dot_general(dpre, w_nbr[...], OVER_COLS, preferred_element_type=F32) / FAN).astype(BF)
    both_v[:NODES, :] = dagg
    both_v[NODES:, :] = dpre
    copies = send([both_v], [both], sems)
    out_v[:, :D] = dot(counts_t[NODES : NODES + HALF, :], dagg).astype(BF)
    out_v[:, D : 2 * D] = dot(counts_t[NODES + HALF : BORDER, :], dagg).astype(BF)
    copies += send([out_v.at[:, : 2 * D]], [outward.at[:, : 2 * D]], sems, 1)
    out_v[:D, 2 * D :] = lax.dot_general(features[...], dpre, OVER_ROWS, preferred_element_type=F32).astype(BF)
    out_v[D:, 2 * D :] = lax.dot_general(agg, dpre, OVER_ROWS, preferred_element_type=F32).astype(BF)
    copies += send([out_v.at[:, 2 * D :]], [outward.at[:, 2 * D :]], sems, 2)
    finished(copies)


def other_hubs(counts_t, both, out):
    out[...] = dot(counts_t[BORDER + SIDE :, :], both[:NODES, :]).astype(BF)


def mine_and_own(counts_t, both, w_self, hubs, own):
    dagg = both[:NODES, :]
    hubs[...] = dot(counts_t[BORDER : BORDER + SIDE, :], dagg).astype(BF)
    own[...] = dot(counts_t[:NODES, :], dagg) + lax.dot_general(
        both[NODES:, :], w_self[...], OVER_COLS, preferred_element_type=F32
    )


def pair_hubs(x, hubs, met, kept, *to):
    for k, out in enumerate((kept,) + to):
        place = lax.rem(x[0] + k, XS)
        rows = pl.ds(pl.multiple_of(place * 256, 256), 256)
        out[...] = (hubs[rows, :].astype(F32) + met[rows, :].astype(F32)).astype(BF)


def sum_hubs(kept, a, b, c, message, tiles, sems):
    total = kept[...].astype(F32) + a[...].astype(F32) + b[...].astype(F32) + c[...].astype(F32)
    tiles[...] = split_rows(total).reshape(HALF, 128).astype(BF)
    finished(send([tiles], [message.at[:, D:]], sems))


def sum_weights(returned, out):
    total = jnp.sum(returned[:, 2 * D :].astype(F32).reshape(MEMBERS, 8, D), axis=0)
    out[...] = jnp.broadcast_to(total[None], (GROUPS, 8, D)).reshape(GROUPS * 8, D).astype(BF)


def add_returned(returned, home, own, out):
    total = own[...] + dot(home[:, :HALF], returned[:, :D])
    out[...] = total + dot(home[:, HALF:], returned[:, D : 2 * D])


def last_message(weights, hubs, message, rows, sems):
    total = jnp.sum(weights[...].astype(F32).reshape(GROUPS, 8, D), axis=0) * SCALE
    rows[...] = jnp.broadcast_to(total[None], (MEMBERS, 8, D)).reshape(HALF, D).astype(BF)
    finished(send([rows], [message.at[:, :D]], sems))


def finish(hub, last, partial, grad_self, grad_nbr, grad, weights_v, grad_v, sems):
    weights_v[...] = last[:, :D].astype(F32)
    copies = send([weights_v.at[:D, :], weights_v.at[D:, :]], [grad_self, grad_nbr], sems)
    tile = jnp.sum(last[:, D:].astype(F32).reshape(MEMBERS, 8, 128), axis=0)
    total = partial[...]
    node = iota((NODES, D), 0)
    for h in range(HUBS):
        row = jnp.concatenate([tile[h : h + 1], tile[h + 4 : h + 5]], axis=1)
        total = total + jnp.where(node == hub_ids(hub[...], (NODES, D), h), row, 0.0)
    grad_v[...] = total.astype(BF)
    copies += send([grad_v], [grad], sems, 2)
    finished(copies)


def exchange(array, axes, parts):
    block = array.reshape(parts, -1, array.shape[1])
    return lax.all_to_all(block, axes, split_axis=0, concat_axis=0, tiled=True).reshape(array.shape)


def local(features, neighbours, send_rows, block_counts, hub_rows, w_self, w_nbr, cotangent):
    core = lax.axis_index("core").reshape(1)
    x = lax.axis_index("x").reshape(1)
    send_t = send_rows.T
    live = block_counts.reshape(1, MEMBERS)
    side = ((SIDE, D), BF)
    (outgoing,) = call(
        outgoing_rows, "outgoing_rows", [((HALF, 640), BF)], 2**27, 2**20,
        hub_rows, send_t, live, features,
        kept=range(4), to_hbm=(0,),
        scratch=[
            pltpu.VMEM((1, HUBS), I32), pltpu.VMEM((SLOTS, MEMBERS), I32), pltpu.VMEM((1, MEMBERS), I32),
            pltpu.VMEM((NODES, D), BF), pltpu.VMEM((HALF, 640), BF), pltpu.SemaphoreType.DMA((7,)),
        ],
    )
    incoming = exchange(outgoing, MEMBER, MEMBERS)
    counts, counts_t, home, pre_self, counted = call(
        count_rows, "count_rows",
        [((NODES, TABLE), BF), ((TABLE, NODES), BF), ((NODES, 2 * HALF), BF), ((NODES, D), F32), ((8, 128), F32)],
        2**30, 2**22,
        core, neighbours.T, send_t, live, features, w_self, outgoing,
        smem=(0,), unread=(6,),
    )
    (mine,) = call(
        own_hubs, "own_hubs", [side], 2**16, 2**19, incoming, counted,
        kept=(0,), unread=(1,), scratch=[pltpu.VMEM((HALF, 128), BF), pltpu.SemaphoreType.DMA((1,))],
    )
    mine = exchange(mine, "x", XS)
    swap = [(0, 1), (1, 0)]
    other = lax.ppermute(mine, "core", swap)
    (near,) = call(near_sum, "near_sum", [((NODES, D), F32)], 2**28, 2**21, counts, features, incoming, mine)
    outward, both = call(
        forward, "forward", [((HALF, 768), BF), ((2 * NODES, D), BF)], 2**29, 2**22,
        counts, counts_t, features, near, other, pre_self, w_nbr, cotangent,
        to_hbm=range(2),
        scratch=[pltpu.VMEM((HALF, 768), BF), pltpu.VMEM((2 * NODES, D), BF), pltpu.SemaphoreType.DMA((3,))],
    )
    returned = exchange(outward, MEMBER, MEMBERS)

    (theirs,) = call(other_hubs, "other_hubs", [side], 2**27, 2**20, counts_t, both)
    met = lax.ppermute(theirs, "core", swap)
    hubs, own = call(mine_and_own, "mine_and_own", [side, ((NODES, D), F32)], 2**28, 2**21, counts_t, both, w_self)
    block = ((NODES, D), BF)
    kept, *to = call(pair_hubs, "pair_hubs", [block] * XS, 2**18, 2**20, x, hubs, met, smem=(0,))
    came = [lax.ppermute(to[k - 1], "x", [(i, (i + k) % XS) for i in range(XS)]) for k in range(1, XS)]
    (hub_tiles,) = call(
        sum_hubs, "sum_hubs", [((HALF, 384), BF)], 2**18, 2**20, kept, *came,
        to_hbm=(0,), scratch=[pltpu.VMEM((HALF, 128), BF), pltpu.SemaphoreType.DMA((1,))],
    )
    (weights,) = call(sum_weights, "sum_weights", [((GROUPS * 8, D), BF)], 2**17, 2**18, returned)
    weights = exchange(weights, GROUP, GROUPS)
    (partial,) = call(add_returned, "add_returned", [((NODES, D), F32)], 2**27, 2**20, returned, home, own)
    (message,) = call(
        last_message, "last_message", [((HALF, 384), BF)], 2**17, 2**18, weights, hub_tiles,
        kept=(1,), to_hbm=(0,), alias={1: 0}, scratch=[pltpu.VMEM((HALF, D), BF), pltpu.SemaphoreType.DMA((1,))],
    )
    last = exchange(message, MEMBER, MEMBERS)
    return tuple(
        call(
            finish, "finish", [((D, D), F32), ((D, D), F32), ((NODES, D), BF)], 2**18, 2**20, hub_rows, last, partial,
            to_hbm=range(3),
            scratch=[pltpu.VMEM((2 * D, D), F32), pltpu.VMEM((NODES, D), BF), pltpu.SemaphoreType.DMA((3,))],
        )
    )


def solution(mesh):
    split = Mesh(mesh.devices.reshape(XS, 2, 8, 8), ALL)
    rows = P(ALL, None)
    in_specs = (rows, rows, rows, P(ALL), rows, P(), P(), rows)
    out_specs = (P(), P(), rows)
    return jax.shard_map(local, mesh=split, in_specs=in_specs, out_specs=out_specs, check_vma=False)
```

```python
import math

import jax
import jax.numpy as jnp
from jax import lax
from jax.experimental import pallas as pl
from jax.experimental.pallas import tpu as pltpu
from jax.sharding import Mesh, PartitionSpec as P

BF = jnp.bfloat16
F32 = jnp.float32
I32 = jnp.int32
GROUP = ("x", "core")
MEMBER = ("y", "z")
ALL = ("x", "core", "y", "z")

D = 256
NODES = 256
FAN = 10
MEMBERS = 64
SLOTS = 16
HUBS = 4
GROUPS = 8
XS = 4
HALF = MEMBERS * 8
BORDER = NODES + 2 * HALF
SIDE = XS * MEMBERS * HUBS
TABLE = BORDER + 2 * SIDE
SCALE = 1.0 / math.sqrt(NODES * GROUPS * MEMBERS)
OVER_ROWS = (((0,), (0,)), ((), ()))
OVER_COLS = (((1,), (1,)), ((), ()))

VMEM = pl.BlockSpec(memory_space=pltpu.VMEM)
SMEM = pl.BlockSpec(memory_space=pltpu.SMEM)
HBM = pl.BlockSpec(memory_space=pltpu.HBM)
ANY = pl.BlockSpec(memory_space=pl.ANY)


def iota(shape, dim):
    return lax.broadcasted_iota(I32, shape, dim)


def dot(a, b):
    return jnp.dot(a, b, preferred_element_type=F32)


def call(body, name, outs, flops, moved, *args, kept=(), smem=(), unread=(), to_hbm=(), scratch=(), alias={}):
    places = [HBM if i in kept else SMEM if i in smem else ANY if i in unread else VMEM for i in range(len(args))]
    return pl.pallas_call(
        body,
        name=name,
        out_shape=[(pltpu.HBM if i in to_hbm else jax.ShapeDtypeStruct)(s, t) for i, (s, t) in enumerate(outs)],
        in_specs=places,
        out_specs=[HBM if i in to_hbm else VMEM for i in range(len(outs))],
        scratch_shapes=list(scratch),
        input_output_aliases=alias,
        compiler_params=pltpu.CompilerParams(vmem_limit_bytes=16 * 1024 * 1024),
        cost_estimate=pl.CostEstimate(flops=flops, bytes_accessed=moved, transcendentals=0),
    )(*[pltpu.with_memory_space_constraint(a, pltpu.HBM) if i in kept else a for i, a in enumerate(args)])


def send(sources, targets, sems, first=0):
    copies = [pltpu.make_async_copy(a, b, sems.at[first + i]) for i, (a, b) in enumerate(zip(sources, targets))]
    for copy in copies:
        copy.start()
    return copies


def finished(copies):
    for copy in copies:
        copy.wait()


def split_rows(rows):
    left = rows[:, :128].reshape(-1, 8, 128)
    right = rows[:, 128:].reshape(-1, 8, 128)
    low = iota(left.shape, 1) < 4
    even = jnp.where(low, left, pltpu.roll(right, 4, 1))
    odd = jnp.where(low, pltpu.roll(left, 4, 1), right)
    return jnp.stack([even, odd], axis=1).reshape(-1, 8, 128)


def join_rows(tiles):
    pairs = tiles.reshape(-1, 2, 8, 128)
    even, odd = pairs[:, 0], pairs[:, 1]
    low = iota(even.shape, 1) < 4
    left = jnp.where(low, even, pltpu.roll(odd, 4, 1)).reshape(-1, 128)
    right = jnp.where(low, pltpu.roll(even, 4, 1), odd).reshape(-1, 128)
    return left, right


def hot_rows(send_t, count):
    own = (iota((HALF, MEMBERS), 0) >> 3) == iota((HALF, MEMBERS), 1)
    spread = lax.dot_general(
        own.astype(F32).astype(BF), send_t.astype(F32).astype(BF), OVER_COLS, preferred_element_type=F32
    )
    live = jnp.sum(jnp.where(own, count.astype(F32), 0.0), axis=1, keepdims=True)
    lane = iota((HALF, SLOTS), 1)
    slot = iota((HALF, SLOTS), 0) & 7
    place = (iota((HALF, 1), 0) & 7).astype(F32)
    nodes = iota((HALF, NODES), 1).astype(F32)
    hot = []
    for a in range(2):
        row = jnp.sum(jnp.where(lane == slot + 8 * a, spread, 0.0), axis=1, keepdims=True)
        row = jnp.where(place + 8.0 * a < live, row, -1.0)
        hot.append((nodes == row).astype(F32).astype(BF))
    return hot


def hub_ids(hub, shape, h):
    return jnp.broadcast_to(jnp.sum(jnp.where(iota(hub.shape, 1) == h, hub, 0), axis=1, keepdims=True), shape)


def outgoing_rows(hub, send_t, count, features, out, hub_v, send_v, count_v, f_v, out_v, sems):
    copies = send((send_t, count, hub, features), (send_v, count_v, hub_v, f_v), sems)
    finished(copies[:2])
    hot = hot_rows(send_v[...], count_v[...])
    finished(copies[2:])
    f = f_v[...]
    which = iota((16, NODES), 0) & 3
    ids = jnp.full((16, NODES), -1, I32)
    for h in range(HUBS):
        ids = jnp.where(which == h, hub_ids(hub_v[...], ids.shape, h), ids)
    rows = dot((ids == iota((16, NODES), 1)).astype(F32).astype(BF), f)
    tile = jnp.where(iota((8, 128), 0) < 4, rows[:8, :128], rows[:8, 128:])
    out_v[:, 2 * D :] = jnp.broadcast_to(tile[None], (MEMBERS, 8, 128)).reshape(HALF, 128).astype(BF)
    copies = send([out_v.at[:, 2 * D :]], [out.at[:, 2 * D :]], sems, 4)
    for a in range(2):
        lanes = slice(a * D, (a + 1) * D)
        out_v[:, lanes] = dot(hot[a], f).astype(BF)
        copies += send([out_v.at[:, lanes]], [out.at[:, lanes]], sems, 5 + a)
    finished(copies)


def table_row(n, core):
    b = n - NODES
    h = b - MEMBERS * SLOTS
    border = NODES + ((b >> 3) & 1) * HALF + (b >> 4) * 8 + (b & 7)
    side = ((h >> 8) & 1) ^ core
    hub = BORDER + side * SIDE + (h >> 9) * 256 + (h & 255)
    return jnp.where(b < 0, n, jnp.where(h < 0, border, hub))


def count_rows(core, near_t, send_t, count, features, w_self, after, counts, counts_out, home, pre_self, done, counts_t, sems):
    row_t = table_row(near_t[...], core[0])
    step = 32

    @pl.loop(0, TABLE // step)
    def _(i):
        base = pl.multiple_of(i * step, step)
        ids = iota((step, NODES), 0) + base
        total = jnp.zeros((step, NODES), F32)
        for f in range(FAN):
            total = total + jnp.where(ids == row_t[f : f + 1, :], 1.0, 0.0)
        counts_t[pl.ds(base, step), :] = total.astype(BF)

    copies = send([counts_t], [counts_out], sems)
    eye = (iota((NODES, NODES), 0) == iota((NODES, NODES), 1)).astype(F32).astype(BF)
    for t in range(TABLE // 256):
        block = lax.dot_general(eye, counts_t[t * 256 : (t + 1) * 256, :], OVER_COLS, preferred_element_type=F32)
        counts[:, t * 256 : (t + 1) * 256] = block.astype(BF)
    for a, hot in enumerate(hot_rows(send_t[...], count[...])):
        block = lax.dot_general(eye, hot, OVER_COLS, preferred_element_type=F32)
        home[:, a * HALF : (a + 1) * HALF] = block.astype(BF)
    pre_self[...] = dot(features[...], w_self[...])
    done[...] = jnp.zeros((8, 128), F32)
    finished(copies)


def own_hubs(incoming, after, out):
    left, right = join_rows(incoming[:, 2 * D :].astype(F32).reshape(MEMBERS, 8, 128))
    left, right = left.astype(BF), right.astype(BF)
    for x in range(XS):
        out[x * 256 : (x + 1) * 256, :128] = left
        out[x * 256 : (x + 1) * 256, 128:] = right


def near_sum(counts, counts_t, features, incoming, mine, out, back, sems):
    fetch = send([counts_t.at[NODES:BORDER, :]], [back], sems)
    total = dot(counts[:, :NODES], features[...])
    total += dot(counts[:, NODES : NODES + HALF], incoming[:, :D])
    total += dot(counts[:, NODES + HALF : BORDER], incoming[:, D : 2 * D])
    out[...] = total + dot(counts[:, BORDER : BORDER + SIDE], mine[...])
    finished(fetch)


def forward(
    counts, back, features, near, other, pre_self, w_nbr, cotangent, outward, both, out_v, both_v, sems
):
    total = near[...] + dot(counts[:, BORDER + SIDE :], other[...])
    agg = (total / FAN).astype(BF)
    pre = pre_self[...] + dot(agg, w_nbr[...])
    sigma = 1.0 / (1.0 + jnp.exp(-pre))
    dpre = (cotangent[...].astype(F32) * sigma * (1.0 + pre * (1.0 - sigma))).astype(BF)
    dagg = (lax.dot_general(dpre, w_nbr[...], OVER_COLS, preferred_element_type=F32) / FAN).astype(BF)
    both_v[:NODES, :] = dagg
    both_v[NODES:, :] = dpre
    copies = send([both_v], [both], sems)
    out_v[:, :D] = dot(back[:HALF, :], dagg).astype(BF)
    out_v[:, D : 2 * D] = dot(back[HALF:, :], dagg).astype(BF)
    copies += send([out_v.at[:, : 2 * D]], [outward.at[:, : 2 * D]], sems, 1)
    out_v[:D, 2 * D :] = lax.dot_general(features[...], dpre, OVER_ROWS, preferred_element_type=F32).astype(BF)
    out_v[D:, 2 * D :] = lax.dot_general(agg, dpre, OVER_ROWS, preferred_element_type=F32).astype(BF)
    copies += send([out_v.at[:, 2 * D :]], [outward.at[:, 2 * D :]], sems, 2)
    finished(copies)


def other_hubs(counts_t, both, out, rows, sems):
    finished(send([counts_t.at[BORDER + SIDE :, :]], [rows], sems))
    out[...] = dot(rows[...], both[:NODES, :]).astype(BF)


def mine_and_own(counts_t, both, w_self, hubs, own, rows, near, sems):
    finished(send([counts_t.at[BORDER : BORDER + SIDE, :], counts_t.at[:NODES, :]], [rows, near], sems))
    dagg = both[:NODES, :]
    hubs[...] = dot(rows[...], dagg).astype(BF)
    own[...] = dot(near[...], dagg) + lax.dot_general(
        both[NODES:, :], w_self[...], OVER_COLS, preferred_element_type=F32
    )


def pair_hubs(x, hubs, met, kept, *to):
    for k, out in enumerate((kept,) + to):
        place = lax.rem(x[0] + k, XS)
        rows = pl.ds(pl.multiple_of(place * 256, 256), 256)
        out[...] = (hubs[rows, :].astype(F32) + met[rows, :].astype(F32)).astype(BF)


def sum_hubs(kept, a, b, c, message, tiles, sems):
    total = kept[...].astype(F32) + a[...].astype(F32) + b[...].astype(F32) + c[...].astype(F32)
    tiles[...] = split_rows(total).reshape(HALF, 128).astype(BF)
    finished(send([tiles], [message.at[:, D:]], sems))


def sum_weights(returned, out):
    total = jnp.sum(returned[:, 2 * D :].astype(F32).reshape(MEMBERS, 8, D), axis=0)
    out[...] = jnp.broadcast_to(total[None], (GROUPS, 8, D)).reshape(GROUPS * 8, D).astype(BF)


def add_returned(returned, home, own, out):
    total = own[...] + dot(home[:, :HALF], returned[:, :D])
    out[...] = total + dot(home[:, HALF:], returned[:, D : 2 * D])


def last_message(weights, hubs, message, rows, sems):
    total = jnp.sum(weights[...].astype(F32).reshape(GROUPS, 8, D), axis=0) * SCALE
    rows[...] = jnp.broadcast_to(total[None], (MEMBERS, 8, D)).reshape(HALF, D).astype(BF)
    finished(send([rows], [message.at[:, :D]], sems))


def finish(hub, last, partial, grad_self, grad_nbr, grad, weights_v, grad_v, sems):
    weights_v[...] = last[:, :D].astype(F32)
    copies = send([weights_v.at[:D, :], weights_v.at[D:, :]], [grad_self, grad_nbr], sems)
    tile = jnp.sum(last[:, D:].astype(F32).reshape(MEMBERS, 8, 128), axis=0)
    total = partial[...]
    node = iota((NODES, D), 0)
    for h in range(HUBS):
        row = jnp.concatenate([tile[h : h + 1], tile[h + 4 : h + 5]], axis=1)
        total = total + jnp.where(node == hub_ids(hub[...], (NODES, D), h), row, 0.0)
    grad_v[...] = total.astype(BF)
    copies += send([grad_v], [grad], sems, 2)
    finished(copies)


def exchange(array, axes, parts):
    block = array.reshape(parts, -1, array.shape[1])
    return lax.all_to_all(block, axes, split_axis=0, concat_axis=0, tiled=True).reshape(array.shape)


def local(features, neighbours, send_rows, block_counts, hub_rows, w_self, w_nbr, cotangent):
    core = lax.axis_index("core").reshape(1)
    x = lax.axis_index("x").reshape(1)
    send_t = send_rows.T
    live = block_counts.reshape(1, MEMBERS)
    side = ((SIDE, D), BF)
    (outgoing,) = call(
        outgoing_rows, "outgoing_rows", [((HALF, 640), BF)], 2**20, 2**23,
        hub_rows, send_t, live, features,
        kept=range(4), to_hbm=(0,),
        scratch=[
            pltpu.VMEM((1, HUBS), I32), pltpu.VMEM((SLOTS, MEMBERS), I32), pltpu.VMEM((1, MEMBERS), I32),
            pltpu.VMEM((NODES, D), BF), pltpu.VMEM((HALF, 640), BF), pltpu.SemaphoreType.DMA((7,)),
        ],
    )
    incoming = exchange(outgoing, MEMBER, MEMBERS)
    counts, counts_t, home, pre_self, counted = call(
        count_rows, "count_rows",
        [((NODES, TABLE), BF), ((TABLE, NODES), BF), ((NODES, 2 * HALF), BF), ((NODES, D), F32), ((8, 128), F32)],
        2**20, 2**23,
        core, neighbours.T, send_t, live, features, w_self, outgoing,
        smem=(0,), kept=(6,), to_hbm=(1,), scratch=[pltpu.VMEM((TABLE, NODES), BF), pltpu.SemaphoreType.DMA((1,))],
    )
    (mine,) = call(own_hubs, "own_hubs", [side], 2**20, 2**23, incoming, counted, unread=(1,))
    mine = exchange(mine, "x", XS)
    swap = [(0, 1), (1, 0)]
    other = lax.ppermute(mine, "core", swap)
    near, back = call(
        near_sum, "near_sum", [((NODES, D), F32), ((2 * HALF, NODES), BF)], 2**20, 2**23,
        counts, counts_t, features, incoming, mine,
        kept=(1,), scratch=[pltpu.SemaphoreType.DMA((1,))],
    )
    outward, both = call(
        forward, "forward", [((HALF, 768), BF), ((2 * NODES, D), BF)], 2**20, 2**23,
        counts, back, features, near, other, pre_self, w_nbr, cotangent,
        to_hbm=range(2),
        scratch=[pltpu.VMEM((HALF, 768), BF), pltpu.VMEM((2 * NODES, D), BF), pltpu.SemaphoreType.DMA((3,))],
    )
    returned = exchange(outward, MEMBER, MEMBERS)

    rows = pltpu.VMEM((SIDE, NODES), BF)
    (theirs,) = call(
        other_hubs, "other_hubs", [side], 2**20, 2**23, counts_t, both,
        kept=(0,), scratch=[rows, pltpu.SemaphoreType.DMA((1,))],
    )
    met = lax.ppermute(theirs, "core", swap)
    hubs, own = call(
        mine_and_own, "mine_and_own", [side, ((NODES, D), F32)], 2**20, 2**23, counts_t, both, w_self,
        kept=(0,), scratch=[rows, pltpu.VMEM((NODES, NODES), BF), pltpu.SemaphoreType.DMA((2,))],
    )
    block = ((NODES, D), BF)
    kept, *to = call(pair_hubs, "pair_hubs", [block] * XS, 2**20, 2**23, x, hubs, met, smem=(0,))
    came = [lax.ppermute(to[k - 1], "x", [(i, (i + k) % XS) for i in range(XS)]) for k in range(1, XS)]
    (hub_tiles,) = call(
        sum_hubs, "sum_hubs", [((HALF, 384), BF)], 2**20, 2**23, kept, *came,
        to_hbm=(0,), scratch=[pltpu.VMEM((HALF, 128), BF), pltpu.SemaphoreType.DMA((1,))],
    )
    (weights,) = call(sum_weights, "sum_weights", [((GROUPS * 8, D), BF)], 2**20, 2**23, returned)
    weights = exchange(weights, GROUP, GROUPS)
    (partial,) = call(add_returned, "add_returned", [((NODES, D), F32)], 2**20, 2**23, returned, home, own)
    (message,) = call(
        last_message, "last_message", [((HALF, 384), BF)], 2**20, 2**23, weights, hub_tiles,
        kept=(1,), to_hbm=(0,), alias={1: 0}, scratch=[pltpu.VMEM((HALF, D), BF), pltpu.SemaphoreType.DMA((1,))],
    )
    last = exchange(message, MEMBER, MEMBERS)
    return tuple(
        call(
            finish, "finish", [((D, D), F32), ((D, D), F32), ((NODES, D), BF)], 2**20, 2**23, hub_rows, last, partial,
            to_hbm=range(3),
            scratch=[pltpu.VMEM((2 * D, D), F32), pltpu.VMEM((NODES, D), BF), pltpu.SemaphoreType.DMA((3,))],
        )
    )


def solution(mesh):
    split = Mesh(mesh.devices.reshape(XS, 2, 8, 8), ALL)
    rows = P(ALL, None)
    in_specs = (rows, rows, rows, P(ALL), rows, P(), P(), rows)
    out_specs = (P(), P(), rows)
    return jax.shard_map(local, mesh=split, in_specs=in_specs, out_specs=out_specs, check_vma=False)
```

```python
import math

import jax
import jax.numpy as jnp
from jax import lax
from jax.experimental import pallas as pl
from jax.experimental.pallas import tpu as pltpu
from jax.sharding import Mesh, PartitionSpec as P

BF = jnp.bfloat16
F32 = jnp.float32
I32 = jnp.int32
GROUP = ("x", "core")
MEMBER = ("y", "z")
ALL = ("x", "core", "y", "z")

D = 256
NODES = 256
FAN = 10
MEMBERS = 64
SLOTS = 16
HUBS = 4
GROUPS = 8
XS = 4
HALF = MEMBERS * 8
BORDER = NODES + 2 * HALF
SIDE = XS * MEMBERS * HUBS
TABLE = BORDER + 2 * SIDE
SCALE = 1.0 / math.sqrt(NODES * GROUPS * MEMBERS)
OVER_ROWS = (((0,), (0,)), ((), ()))
OVER_COLS = (((1,), (1,)), ((), ()))

VMEM = pl.BlockSpec(memory_space=pltpu.VMEM)
SMEM = pl.BlockSpec(memory_space=pltpu.SMEM)
HBM = pl.BlockSpec(memory_space=pltpu.HBM)
ANY = pl.BlockSpec(memory_space=pl.ANY)


def iota(shape, dim):
    return lax.broadcasted_iota(I32, shape, dim)


def dot(a, b):
    return jnp.dot(a, b, preferred_element_type=F32)


def call(body, name, outs, flops, moved, *args, kept=(), smem=(), unread=(), to_hbm=(), scratch=()):
    places = [HBM if i in kept else SMEM if i in smem else ANY if i in unread else VMEM for i in range(len(args))]
    return pl.pallas_call(
        body,
        name=name,
        out_shape=[(pltpu.HBM if i in to_hbm else jax.ShapeDtypeStruct)(s, t) for i, (s, t) in enumerate(outs)],
        in_specs=places,
        out_specs=[HBM if i in to_hbm else VMEM for i in range(len(outs))],
        scratch_shapes=list(scratch),
        compiler_params=pltpu.CompilerParams(vmem_limit_bytes=16 * 1024 * 1024),
        cost_estimate=pl.CostEstimate(flops=flops, bytes_accessed=moved, transcendentals=0),
    )(*[pltpu.with_memory_space_constraint(a, pltpu.HBM) if i in kept else a for i, a in enumerate(args)])


def send(sources, targets, sems, first=0):
    copies = [pltpu.make_async_copy(a, b, sems.at[first + i]) for i, (a, b) in enumerate(zip(sources, targets))]
    for copy in copies:
        copy.start()
    return copies


def finished(copies):
    for copy in copies:
        copy.wait()


def split_rows(rows):
    left = rows[:, :128].reshape(-1, 8, 128)
    right = rows[:, 128:].reshape(-1, 8, 128)
    low = iota(left.shape, 1) < 4
    even = jnp.where(low, left, pltpu.roll(right, 4, 1))
    odd = jnp.where(low, pltpu.roll(left, 4, 1), right)
    return jnp.stack([even, odd], axis=1).reshape(-1, 8, 128)


def join_rows(tiles):
    pairs = tiles.reshape(-1, 2, 8, 128)
    even, odd = pairs[:, 0], pairs[:, 1]
    low = iota(even.shape, 1) < 4
    left = jnp.where(low, even, pltpu.roll(odd, 4, 1)).reshape(-1, 128)
    right = jnp.where(low, pltpu.roll(even, 4, 1), odd).reshape(-1, 128)
    return left, right


def hot_rows(send_t, count):
    own = (iota((HALF, MEMBERS), 0) >> 3) == iota((HALF, MEMBERS), 1)
    spread = lax.dot_general(
        own.astype(F32).astype(BF), send_t.astype(F32).astype(BF), OVER_COLS, preferred_element_type=F32
    )
    live = jnp.sum(jnp.where(own, count.astype(F32), 0.0), axis=1, keepdims=True)
    lane = iota((HALF, SLOTS), 1)
    slot = iota((HALF, SLOTS), 0) & 7
    place = (iota((HALF, 1), 0) & 7).astype(F32)
    nodes = iota((HALF, NODES), 1).astype(F32)
    hot = []
    for a in range(2):
        row = jnp.sum(jnp.where(lane == slot + 8 * a, spread, 0.0), axis=1, keepdims=True)
        row = jnp.where(place + 8.0 * a < live, row, -1.0)
        hot.append((nodes == row).astype(F32).astype(BF))
    return hot


def hub_ids(hub, shape, h):
    return jnp.broadcast_to(jnp.sum(jnp.where(iota(hub.shape, 1) == h, hub, 0), axis=1, keepdims=True), shape)


def outgoing_rows(hub, send_t, count, features, out, hub_v, send_v, count_v, f_v, out_v, sems):
    copies = send((send_t, count, hub, features), (send_v, count_v, hub_v, f_v), sems)
    finished(copies[:2])
    hot = hot_rows(send_v[...], count_v[...])
    finished(copies[2:])
    f = f_v[...]
    which = iota((16, NODES), 0) & 3
    ids = jnp.full((16, NODES), -1, I32)
    for h in range(HUBS):
        ids = jnp.where(which == h, hub_ids(hub_v[...], ids.shape, h), ids)
    rows = dot((ids == iota((16, NODES), 1)).astype(F32).astype(BF), f)
    tile = jnp.where(iota((8, 128), 0) < 4, rows[:8, :128], rows[:8, 128:])
    out_v[:, 2 * D :] = jnp.broadcast_to(tile[None], (MEMBERS, 8, 128)).reshape(HALF, 128).astype(BF)
    copies = send([out_v.at[:, 2 * D :]], [out.at[:, 2 * D :]], sems, 4)
    for a in range(2):
        lanes = slice(a * D, (a + 1) * D)
        out_v[:, lanes] = dot(hot[a], f).astype(BF)
        copies += send([out_v.at[:, lanes]], [out.at[:, lanes]], sems, 5 + a)
    finished(copies)


def table_row(n, core):
    b = n - NODES
    h = b - MEMBERS * SLOTS
    border = NODES + ((b >> 3) & 1) * HALF + (b >> 4) * 8 + (b & 7)
    side = ((h >> 8) & 1) ^ core
    hub = BORDER + side * SIDE + (h >> 9) * 256 + (h & 255)
    return jnp.where(b < 0, n, jnp.where(h < 0, border, hub))


def count_rows(core, near_t, send_t, count, features, w_self, after, counts, counts_out, home, pre_self, done, counts_t, sems):
    row_t = table_row(near_t[...], core[0])
    step = 32

    @pl.loop(0, TABLE // step)
    def _(i):
        base = pl.multiple_of(i * step, step)
        ids = iota((step, NODES), 0) + base
        total = jnp.zeros((step, NODES), F32)
        for f in range(FAN):
            total = total + jnp.where(ids == row_t[f : f + 1, :], 1.0, 0.0)
        counts_t[pl.ds(base, step), :] = total.astype(BF)

    copies = send([counts_t], [counts_out], sems)
    eye = (iota((NODES, NODES), 0) == iota((NODES, NODES), 1)).astype(F32).astype(BF)
    for t in range(TABLE // 256):
        block = lax.dot_general(eye, counts_t[t * 256 : (t + 1) * 256, :], OVER_COLS, preferred_element_type=F32)
        counts[:, t * 256 : (t + 1) * 256] = block.astype(BF)
    for a, hot in enumerate(hot_rows(send_t[...], count[...])):
        block = lax.dot_general(eye, hot, OVER_COLS, preferred_element_type=F32)
        home[:, a * HALF : (a + 1) * HALF] = block.astype(BF)
    pre_self[...] = dot(features[...], w_self[...])
    done[...] = jnp.zeros((8, 128), F32)
    finished(copies)


def own_hubs(incoming, after, out):
    left, right = join_rows(incoming[:, 2 * D :].astype(F32).reshape(MEMBERS, 8, 128))
    left, right = left.astype(BF), right.astype(BF)
    for x in range(XS):
        out[x * 256 : (x + 1) * 256, :128] = left
        out[x * 256 : (x + 1) * 256, 128:] = right


def border_sum(counts, features, incoming, out):
    total = dot(counts[:, :NODES], features[...])
    total += dot(counts[:, NODES : NODES + HALF], incoming[:, :D])
    out[...] = total + dot(counts[:, NODES + HALF : BORDER], incoming[:, D : 2 * D])


def near_sum(counts, counts_t, border, mine, out, back, sems):
    fetch = send([counts_t.at[NODES:BORDER, :]], [back], sems)
    out[...] = border[...] + dot(counts[:, BORDER : BORDER + SIDE], mine[...])
    finished(fetch)


def forward(
    counts, back, features, near, other, pre_self, w_nbr, cotangent, outward, both, out_v, both_v, sems
):
    total = near[...] + dot(counts[:, BORDER + SIDE :], other[...])
    agg = (total / FAN).astype(BF)
    pre = pre_self[...] + dot(agg, w_nbr[...])
    sigma = 1.0 / (1.0 + jnp.exp(-pre))
    dpre = (cotangent[...].astype(F32) * sigma * (1.0 + pre * (1.0 - sigma))).astype(BF)
    dagg = (lax.dot_general(dpre, w_nbr[...], OVER_COLS, preferred_element_type=F32) / FAN).astype(BF)
    both_v[:NODES, :] = dagg
    both_v[NODES:, :] = dpre
    copies = send([both_v], [both], sems)
    out_v[:, :D] = dot(back[:HALF, :], dagg).astype(BF)
    out_v[:, D : 2 * D] = dot(back[HALF:, :], dagg).astype(BF)
    copies += send([out_v.at[:, : 2 * D]], [outward.at[:, : 2 * D]], sems, 1)
    out_v[:D, 2 * D :] = lax.dot_general(features[...], dpre, OVER_ROWS, preferred_element_type=F32).astype(BF)
    out_v[D:, 2 * D :] = lax.dot_general(agg, dpre, OVER_ROWS, preferred_element_type=F32).astype(BF)
    copies += send([out_v.at[:, 2 * D :]], [outward.at[:, 2 * D :]], sems, 2)
    finished(copies)


def other_hubs(counts_t, both, out, rows, sems):
    finished(send([counts_t.at[BORDER + SIDE :, :]], [rows], sems))
    out[...] = dot(rows[...], both[:NODES, :]).astype(BF)


def mine_and_own(counts_t, both, w_self, hubs, own, rows, near, sems):
    finished(send([counts_t.at[BORDER : BORDER + SIDE, :], counts_t.at[:NODES, :]], [rows, near], sems))
    dagg = both[:NODES, :]
    hubs[...] = dot(rows[...], dagg).astype(BF)
    own[...] = dot(near[...], dagg) + lax.dot_general(
        both[NODES:, :], w_self[...], OVER_COLS, preferred_element_type=F32
    )


def pair_hubs(x, hubs, met, kept, *to):
    for k, out in enumerate((kept,) + to):
        place = lax.rem(x[0] + k, XS)
        rows = pl.ds(pl.multiple_of(place * 256, 256), 256)
        out[...] = (hubs[rows, :].astype(F32) + met[rows, :].astype(F32)).astype(BF)


def sum_hubs(kept, a, b, c, out):
    total = kept[...].astype(F32) + a[...].astype(F32) + b[...].astype(F32) + c[...].astype(F32)
    out[...] = split_rows(total).reshape(HALF, 128).astype(BF)


def sum_weights(returned, out):
    total = jnp.sum(returned[:, 2 * D :].astype(F32).reshape(MEMBERS, 8, D), axis=0)
    out[...] = jnp.broadcast_to(total[None], (GROUPS, 8, D)).reshape(GROUPS * 8, D).astype(BF)


def add_returned(returned, home, own, out):
    total = own[...] + dot(home[:, :HALF], returned[:, :D])
    out[...] = total + dot(home[:, HALF:], returned[:, D : 2 * D])


def last_message(weights, hubs, after, out):
    total = jnp.sum(weights[...].astype(F32).reshape(GROUPS, 8, D), axis=0) * SCALE
    out[:, :D] = jnp.broadcast_to(total[None], (MEMBERS, 8, D)).reshape(HALF, D).astype(BF)
    out[:, D:] = hubs[...]


def finish(hub, last, partial, grad_self, grad_nbr, grad, weights_v, grad_v, sems):
    weights_v[...] = last[:, :D].astype(F32)
    copies = send([weights_v.at[:D, :], weights_v.at[D:, :]], [grad_self, grad_nbr], sems)
    tile = jnp.sum(last[:, D:].astype(F32).reshape(MEMBERS, 8, 128), axis=0)
    total = partial[...]
    node = iota((NODES, D), 0)
    for h in range(HUBS):
        row = jnp.concatenate([tile[h : h + 1], tile[h + 4 : h + 5]], axis=1)
        total = total + jnp.where(node == hub_ids(hub[...], (NODES, D), h), row, 0.0)
    grad_v[...] = total.astype(BF)
    copies += send([grad_v], [grad], sems, 2)
    finished(copies)


def exchange(array, axes, parts):
    block = array.reshape(parts, -1, array.shape[1])
    return lax.all_to_all(block, axes, split_axis=0, concat_axis=0, tiled=True).reshape(array.shape)


def local(features, neighbours, send_rows, block_counts, hub_rows, w_self, w_nbr, cotangent):
    core = lax.axis_index("core").reshape(1)
    x = lax.axis_index("x").reshape(1)
    send_t = send_rows.T
    live = block_counts.reshape(1, MEMBERS)
    side = ((SIDE, D), BF)
    (outgoing,) = call(
        outgoing_rows, "outgoing_rows", [((HALF, 640), BF)], 2**20, 2**23,
        hub_rows, send_t, live, features,
        kept=range(4), to_hbm=(0,),
        scratch=[
            pltpu.VMEM((1, HUBS), I32), pltpu.VMEM((SLOTS, MEMBERS), I32), pltpu.VMEM((1, MEMBERS), I32),
            pltpu.VMEM((NODES, D), BF), pltpu.VMEM((HALF, 640), BF), pltpu.SemaphoreType.DMA((7,)),
        ],
    )
    incoming = exchange(outgoing, MEMBER, MEMBERS)
    counts, counts_t, home, pre_self, counted = call(
        count_rows, "count_rows",
        [((NODES, TABLE), BF), ((TABLE, NODES), BF), ((NODES, 2 * HALF), BF), ((NODES, D), F32), ((8, 128), F32)],
        2**20, 2**23,
        core, neighbours.T, send_t, live, features, w_self, outgoing,
        smem=(0,), kept=(6,), to_hbm=(1,), scratch=[pltpu.VMEM((TABLE, NODES), BF), pltpu.SemaphoreType.DMA((1,))],
    )
    (mine,) = call(own_hubs, "own_hubs", [side], 2**20, 2**23, incoming, counted, unread=(1,))
    mine = exchange(mine, "x", XS)
    swap = [(0, 1), (1, 0)]
    other = lax.ppermute(mine, "core", swap)
    (border,) = call(border_sum, "border_sum", [((NODES, D), F32)], 2**20, 2**23, counts, features, incoming)
    near, back = call(
        near_sum, "near_sum", [((NODES, D), F32), ((2 * HALF, NODES), BF)], 2**20, 2**23,
        counts, counts_t, border, mine,
        kept=(1,), scratch=[pltpu.SemaphoreType.DMA((1,))],
    )
    outward, both = call(
        forward, "forward", [((HALF, 768), BF), ((2 * NODES, D), BF)], 2**20, 2**23,
        counts, back, features, near, other, pre_self, w_nbr, cotangent,
        to_hbm=range(2),
        scratch=[pltpu.VMEM((HALF, 768), BF), pltpu.VMEM((2 * NODES, D), BF), pltpu.SemaphoreType.DMA((3,))],
    )
    returned = exchange(outward, MEMBER, MEMBERS)

    rows = pltpu.VMEM((SIDE, NODES), BF)
    (theirs,) = call(
        other_hubs, "other_hubs", [side], 2**20, 2**23, counts_t, both,
        kept=(0,), scratch=[rows, pltpu.SemaphoreType.DMA((1,))],
    )
    met = lax.ppermute(theirs, "core", swap)
    hubs, own = call(
        mine_and_own, "mine_and_own", [side, ((NODES, D), F32)], 2**20, 2**23, counts_t, both, w_self,
        kept=(0,), scratch=[rows, pltpu.VMEM((NODES, NODES), BF), pltpu.SemaphoreType.DMA((2,))],
    )
    block = ((NODES, D), BF)
    kept, *to = call(pair_hubs, "pair_hubs", [block] * XS, 2**20, 2**23, x, hubs, met, smem=(0,))
    came = [lax.ppermute(to[k - 1], "x", [(i, (i + k) % XS) for i in range(XS)]) for k in range(1, XS)]
    (hub_tiles,) = call(sum_hubs, "sum_hubs", [((HALF, 128), BF)], 2**20, 2**23, kept, *came)

    (weights,) = call(sum_weights, "sum_weights", [((GROUPS * 8, D), BF)], 2**20, 2**23, returned)
    weights = exchange(weights, GROUP, GROUPS)
    (partial,) = call(add_returned, "add_returned", [((NODES, D), F32)], 2**20, 2**23, returned, home, own)
    (message,) = call(
        last_message, "last_message", [((HALF, 384), BF)], 2**20, 2**23, weights, hub_tiles, partial, unread=(2,)
    )
    last = exchange(message, MEMBER, MEMBERS)
    return tuple(
        call(
            finish, "finish", [((D, D), F32), ((D, D), F32), ((NODES, D), BF)], 2**20, 2**23, hub_rows, last, partial,
            to_hbm=range(3),
            scratch=[pltpu.VMEM((2 * D, D), F32), pltpu.VMEM((NODES, D), BF), pltpu.SemaphoreType.DMA((3,))],
        )
    )


def solution(mesh):
    split = Mesh(mesh.devices.reshape(XS, 2, 8, 8), ALL)
    rows = P(ALL, None)
    in_specs = (rows, rows, rows, P(ALL), rows, P(), P(), rows)
    out_specs = (P(), P(), rows)
    return jax.shard_map(local, mesh=split, in_specs=in_specs, out_specs=out_specs, check_vma=False)
```

```python
import math

import jax
import jax.numpy as jnp
from jax import lax
from jax.experimental import pallas as pl
from jax.experimental.pallas import tpu as pltpu
from jax.sharding import Mesh, PartitionSpec as P

BF = jnp.bfloat16
F32 = jnp.float32
I32 = jnp.int32
GROUP = ("x", "core")
MEMBER = ("y", "z")
ALL = ("x", "core", "y", "z")

D = 256
NODES = 256
FAN = 10
MEMBERS = 64
SLOTS = 16
HUBS = 4
GROUPS = 8
XS = 4
HALF = MEMBERS * 8
BORDER = NODES + 2 * HALF
SIDE = XS * MEMBERS * HUBS
TABLE = BORDER + 2 * SIDE
SCALE = 1.0 / math.sqrt(NODES * GROUPS * MEMBERS)
OVER_ROWS = (((0,), (0,)), ((), ()))
OVER_COLS = (((1,), (1,)), ((), ()))

VMEM = pl.BlockSpec(memory_space=pltpu.VMEM)
SMEM = pl.BlockSpec(memory_space=pltpu.SMEM)
HBM = pl.BlockSpec(memory_space=pltpu.HBM)
ANY = pl.BlockSpec(memory_space=pl.ANY)


def iota(shape, dim):
    return lax.broadcasted_iota(I32, shape, dim)


def dot(a, b):
    return jnp.dot(a, b, preferred_element_type=F32)


def call(body, name, outs, flops, moved, *args, kept=(), smem=(), unread=(), to_hbm=(), scratch=()):
    places = [HBM if i in kept else SMEM if i in smem else ANY if i in unread else VMEM for i in range(len(args))]
    return pl.pallas_call(
        body,
        name=name,
        out_shape=[(pltpu.HBM if i in to_hbm else jax.ShapeDtypeStruct)(s, t) for i, (s, t) in enumerate(outs)],
        in_specs=places,
        out_specs=[HBM if i in to_hbm else VMEM for i in range(len(outs))],
        scratch_shapes=list(scratch),
        compiler_params=pltpu.CompilerParams(vmem_limit_bytes=16 * 1024 * 1024),
        cost_estimate=pl.CostEstimate(flops=flops, bytes_accessed=moved, transcendentals=0),
    )(*[pltpu.with_memory_space_constraint(a, pltpu.HBM) if i in kept else a for i, a in enumerate(args)])


def send(sources, targets, sems, first=0):
    copies = [pltpu.make_async_copy(a, b, sems.at[first + i]) for i, (a, b) in enumerate(zip(sources, targets))]
    for copy in copies:
        copy.start()
    return copies


def send_rows_out(source, target, sems, first, parts):
    rows = source.shape[0] // parts
    cuts = [slice(i * rows, (i + 1) * rows) for i in range(parts)]
    return send([source.at[c, :] for c in cuts], [target.at[c, :] for c in cuts], sems, first)


def finished(copies):
    for copy in copies:
        copy.wait()


def split_rows(rows):
    left = rows[:, :128].reshape(-1, 8, 128)
    right = rows[:, 128:].reshape(-1, 8, 128)
    low = iota(left.shape, 1) < 4
    even = jnp.where(low, left, pltpu.roll(right, 4, 1))
    odd = jnp.where(low, pltpu.roll(left, 4, 1), right)
    return jnp.stack([even, odd], axis=1).reshape(-1, 8, 128)


def join_rows(tiles):
    pairs = tiles.reshape(-1, 2, 8, 128)
    even, odd = pairs[:, 0], pairs[:, 1]
    low = iota(even.shape, 1) < 4
    left = jnp.where(low, even, pltpu.roll(odd, 4, 1)).reshape(-1, 128)
    right = jnp.where(low, pltpu.roll(even, 4, 1), odd).reshape(-1, 128)
    return left, right


def hot_rows(send_t, count):
    own = (iota((HALF, MEMBERS), 0) >> 3) == iota((HALF, MEMBERS), 1)
    spread = lax.dot_general(
        own.astype(F32).astype(BF), send_t.astype(F32).astype(BF), OVER_COLS, preferred_element_type=F32
    )
    live = jnp.sum(jnp.where(own, count.astype(F32), 0.0), axis=1, keepdims=True)
    lane = iota((HALF, SLOTS), 1)
    slot = iota((HALF, SLOTS), 0) & 7
    place = (iota((HALF, 1), 0) & 7).astype(F32)
    nodes = iota((HALF, NODES), 1).astype(F32)
    hot = []
    for a in range(2):
        row = jnp.sum(jnp.where(lane == slot + 8 * a, spread, 0.0), axis=1, keepdims=True)
        row = jnp.where(place + 8.0 * a < live, row, -1.0)
        hot.append((nodes == row).astype(F32).astype(BF))
    return hot


def hub_ids(hub, shape, h):
    return jnp.broadcast_to(jnp.sum(jnp.where(iota(hub.shape, 1) == h, hub, 0), axis=1, keepdims=True), shape)


def outgoing_rows(hub, send_t, count, features, out, hub_v, send_v, count_v, f_v, out_v, sems):
    copies = send((send_t, count, hub, features), (send_v, count_v, hub_v, f_v), sems)
    finished(copies[:2])
    hot = hot_rows(send_v[...], count_v[...])
    finished(copies[2:])
    f = f_v[...]
    which = iota((16, NODES), 0) & 3
    ids = jnp.full((16, NODES), -1, I32)
    for h in range(HUBS):
        ids = jnp.where(which == h, hub_ids(hub_v[...], ids.shape, h), ids)
    rows = dot((ids == iota((16, NODES), 1)).astype(F32).astype(BF), f)
    tile = jnp.where(iota((8, 128), 0) < 4, rows[:8, :128], rows[:8, 128:])
    out_v[:, 2 * D :] = jnp.broadcast_to(tile[None], (MEMBERS, 8, 128)).reshape(HALF, 128).astype(BF)
    copies = send([out_v.at[:, 2 * D :]], [out.at[:, 2 * D :]], sems, 4)
    for a in range(2):
        lanes = slice(a * D, (a + 1) * D)
        out_v[:, lanes] = dot(hot[a], f).astype(BF)
        copies += send_rows_out(out_v.at[:, lanes], out.at[:, lanes], sems, 5 + 4 * a, 4)
    finished(copies)


def table_row(n, core):
    b = n - NODES
    h = b - MEMBERS * SLOTS
    border = NODES + ((b >> 3) & 1) * HALF + (b >> 4) * 8 + (b & 7)
    side = ((h >> 8) & 1) ^ core
    hub = BORDER + side * SIDE + (h >> 9) * 256 + (h & 255)
    return jnp.where(b < 0, n, jnp.where(h < 0, border, hub))


def count_rows(core, near_t, send_t, count, features, w_self, after, counts, counts_out, home, pre_self, done, counts_t, sems):
    row_t = table_row(near_t[...], core[0])
    step = 32

    @pl.loop(0, TABLE // step)
    def _(i):
        base = pl.multiple_of(i * step, step)
        ids = iota((step, NODES), 0) + base
        total = jnp.zeros((step, NODES), F32)
        for f in range(FAN):
            total = total + jnp.where(ids == row_t[f : f + 1, :], 1.0, 0.0)
        counts_t[pl.ds(base, step), :] = total.astype(BF)

    copies = send([counts_t], [counts_out], sems)
    eye = (iota((NODES, NODES), 0) == iota((NODES, NODES), 1)).astype(F32).astype(BF)
    for t in range(TABLE // 256):
        block = lax.dot_general(eye, counts_t[t * 256 : (t + 1) * 256, :], OVER_COLS, preferred_element_type=F32)
        counts[:, t * 256 : (t + 1) * 256] = block.astype(BF)
    for a, hot in enumerate(hot_rows(send_t[...], count[...])):
        block = lax.dot_general(eye, hot, OVER_COLS, preferred_element_type=F32)
        home[:, a * HALF : (a + 1) * HALF] = block.astype(BF)
    pre_self[...] = dot(features[...], w_self[...])
    done[...] = jnp.zeros((8, 128), F32)
    finished(copies)


def own_hubs(incoming, after, out):
    left, right = join_rows(incoming[:, 2 * D :].astype(F32).reshape(MEMBERS, 8, 128))
    left, right = left.astype(BF), right.astype(BF)
    for x in range(XS):
        out[x * 256 : (x + 1) * 256, :128] = left
        out[x * 256 : (x + 1) * 256, 128:] = right


def border_sum(counts, features, incoming, out):
    total = dot(counts[:, :NODES], features[...])
    total += dot(counts[:, NODES : NODES + HALF], incoming[:, :D])
    out[...] = total + dot(counts[:, NODES + HALF : BORDER], incoming[:, D : 2 * D])


def near_sum(counts, counts_t, border, mine, out, back, sems):
    fetch = send([counts_t.at[NODES:BORDER, :]], [back], sems)
    out[...] = border[...] + dot(counts[:, BORDER : BORDER + SIDE], mine[...])
    finished(fetch)


def forward(
    counts, back, features, near, other, pre_self, w_nbr, cotangent, outward, both, out_v, both_v, sems
):
    total = near[...] + dot(counts[:, BORDER + SIDE :], other[...])
    agg = (total / FAN).astype(BF)
    pre = pre_self[...] + dot(agg, w_nbr[...])
    sigma = 1.0 / (1.0 + jnp.exp(-pre))
    dpre = (cotangent[...].astype(F32) * sigma * (1.0 + pre * (1.0 - sigma))).astype(BF)
    dagg = (lax.dot_general(dpre, w_nbr[...], OVER_COLS, preferred_element_type=F32) / FAN).astype(BF)
    both_v[:NODES, :] = dagg
    both_v[NODES:, :] = dpre
    copies = send([both_v], [both], sems)
    out_v[:, :D] = dot(back[:HALF, :], dagg).astype(BF)
    out_v[:, D : 2 * D] = dot(back[HALF:, :], dagg).astype(BF)
    copies += send_rows_out(out_v.at[:, : 2 * D], outward.at[:, : 2 * D], sems, 1, 4)
    out_v[:D, 2 * D :] = lax.dot_general(features[...], dpre, OVER_ROWS, preferred_element_type=F32).astype(BF)
    out_v[D:, 2 * D :] = lax.dot_general(agg, dpre, OVER_ROWS, preferred_element_type=F32).astype(BF)
    copies += send_rows_out(out_v.at[:, 2 * D :], outward.at[:, 2 * D :], sems, 5, 4)
    finished(copies)


def other_hubs(counts_t, both, out, rows, sems):
    finished(send([counts_t.at[BORDER + SIDE :, :]], [rows], sems))
    out[...] = dot(rows[...], both[:NODES, :]).astype(BF)


def mine_and_own(counts_t, both, w_self, hubs, own, rows, near, sems):
    finished(send([counts_t.at[BORDER : BORDER + SIDE, :], counts_t.at[:NODES, :]], [rows, near], sems))
    dagg = both[:NODES, :]
    hubs[...] = dot(rows[...], dagg).astype(BF)
    own[...] = dot(near[...], dagg) + lax.dot_general(
        both[NODES:, :], w_self[...], OVER_COLS, preferred_element_type=F32
    )


def pair_hubs(x, hubs, met, kept, *to):
    for k, out in enumerate((kept,) + to):
        place = lax.rem(x[0] + k, XS)
        rows = pl.ds(pl.multiple_of(place * 256, 256), 256)
        out[...] = (hubs[rows, :].astype(F32) + met[rows, :].astype(F32)).astype(BF)


def sum_hubs(kept, a, b, c, out):
    total = kept[...].astype(F32) + a[...].astype(F32) + b[...].astype(F32) + c[...].astype(F32)
    out[...] = split_rows(total).reshape(HALF, 128).astype(BF)


def sum_weights(returned, out):
    total = jnp.sum(returned[:, 2 * D :].astype(F32).reshape(MEMBERS, 8, D), axis=0)
    out[...] = jnp.broadcast_to(total[None], (GROUPS, 8, D)).reshape(GROUPS * 8, D).astype(BF)


def add_returned(returned, home, own, out):
    total = own[...] + dot(home[:, :HALF], returned[:, :D])
    out[...] = total + dot(home[:, HALF:], returned[:, D : 2 * D])


def last_message(weights, hubs, after, out):
    total = jnp.sum(weights[...].astype(F32).reshape(GROUPS, 8, D), axis=0) * SCALE
    out[:, :D] = jnp.broadcast_to(total[None], (MEMBERS, 8, D)).reshape(HALF, D).astype(BF)
    out[:, D:] = hubs[...]


def finish(hub, last, partial, grad_self, grad_nbr, grad, weights_v, grad_v, sems):
    weights_v[...] = last[:, :D].astype(F32)
    copies = send([weights_v.at[:D, :], weights_v.at[D:, :]], [grad_self, grad_nbr], sems)
    tile = jnp.sum(last[:, D:].astype(F32).reshape(MEMBERS, 8, 128), axis=0)
    total = partial[...]
    node = iota((NODES, D), 0)
    for h in range(HUBS):
        row = jnp.concatenate([tile[h : h + 1], tile[h + 4 : h + 5]], axis=1)
        total = total + jnp.where(node == hub_ids(hub[...], (NODES, D), h), row, 0.0)
    grad_v[...] = total.astype(BF)
    copies += send([grad_v], [grad], sems, 2)
    finished(copies)


def exchange(array, axes, parts):
    block = array.reshape(parts, -1, array.shape[1])
    return lax.all_to_all(block, axes, split_axis=0, concat_axis=0, tiled=True).reshape(array.shape)


def local(features, neighbours, send_rows, block_counts, hub_rows, w_self, w_nbr, cotangent):
    core = lax.axis_index("core").reshape(1)
    x = lax.axis_index("x").reshape(1)
    send_t = send_rows.T
    live = block_counts.reshape(1, MEMBERS)
    side = ((SIDE, D), BF)
    (outgoing,) = call(
        outgoing_rows, "outgoing_rows", [((HALF, 640), BF)], 2**20, 2**23,
        hub_rows, send_t, live, features,
        kept=range(4), to_hbm=(0,),
        scratch=[
            pltpu.VMEM((1, HUBS), I32), pltpu.VMEM((SLOTS, MEMBERS), I32), pltpu.VMEM((1, MEMBERS), I32),
            pltpu.VMEM((NODES, D), BF), pltpu.VMEM((HALF, 640), BF), pltpu.SemaphoreType.DMA((13,)),
        ],
    )
    incoming = exchange(outgoing, MEMBER, MEMBERS)
    counts, counts_t, home, pre_self, counted = call(
        count_rows, "count_rows",
        [((NODES, TABLE), BF), ((TABLE, NODES), BF), ((NODES, 2 * HALF), BF), ((NODES, D), F32), ((8, 128), F32)],
        2**20, 2**23,
        core, neighbours.T, send_t, live, features, w_self, outgoing,
        smem=(0,), kept=(6,), to_hbm=(1,), scratch=[pltpu.VMEM((TABLE, NODES), BF), pltpu.SemaphoreType.DMA((1,))],
    )
    (mine,) = call(own_hubs, "own_hubs", [side], 2**20, 2**23, incoming, counted, unread=(1,))
    mine = exchange(mine, "x", XS)
    swap = [(0, 1), (1, 0)]
    other = lax.ppermute(mine, "core", swap)
    (border,) = call(border_sum, "border_sum", [((NODES, D), F32)], 2**20, 2**23, counts, features, incoming)
    near, back = call(
        near_sum, "near_sum", [((NODES, D), F32), ((2 * HALF, NODES), BF)], 2**20, 2**23,
        counts, counts_t, border, mine,
        kept=(1,), scratch=[pltpu.SemaphoreType.DMA((1,))],
    )
    outward, both = call(
        forward, "forward", [((HALF, 768), BF), ((2 * NODES, D), BF)], 2**20, 2**23,
        counts, back, features, near, other, pre_self, w_nbr, cotangent,
        to_hbm=range(2),
        scratch=[pltpu.VMEM((HALF, 768), BF), pltpu.VMEM((2 * NODES, D), BF), pltpu.SemaphoreType.DMA((9,))],
    )
    returned = exchange(outward, MEMBER, MEMBERS)

    rows = pltpu.VMEM((SIDE, NODES), BF)
    (theirs,) = call(
        other_hubs, "other_hubs", [side], 2**20, 2**23, counts_t, both,
        kept=(0,), scratch=[rows, pltpu.SemaphoreType.DMA((1,))],
    )
    met = lax.ppermute(theirs, "core", swap)
    hubs, own = call(
        mine_and_own, "mine_and_own", [side, ((NODES, D), F32)], 2**20, 2**23, counts_t, both, w_self,
        kept=(0,), scratch=[rows, pltpu.VMEM((NODES, NODES), BF), pltpu.SemaphoreType.DMA((2,))],
    )
    block = ((NODES, D), BF)
    kept, *to = call(pair_hubs, "pair_hubs", [block] * XS, 2**20, 2**23, x, hubs, met, smem=(0,))
    came = [lax.ppermute(to[k - 1], "x", [(i, (i + k) % XS) for i in range(XS)]) for k in range(1, XS)]
    (hub_tiles,) = call(sum_hubs, "sum_hubs", [((HALF, 128), BF)], 2**20, 2**23, kept, *came)

    (weights,) = call(sum_weights, "sum_weights", [((GROUPS * 8, D), BF)], 2**20, 2**23, returned)
    weights = exchange(weights, GROUP, GROUPS)
    (partial,) = call(add_returned, "add_returned", [((NODES, D), F32)], 2**20, 2**23, returned, home, own)
    (message,) = call(
        last_message, "last_message", [((HALF, 384), BF)], 2**20, 2**23, weights, hub_tiles, partial, unread=(2,)
    )
    last = exchange(message, MEMBER, MEMBERS)
    return tuple(
        call(
            finish, "finish", [((D, D), F32), ((D, D), F32), ((NODES, D), BF)], 2**20, 2**23, hub_rows, last, partial,
            to_hbm=range(3),
            scratch=[pltpu.VMEM((2 * D, D), F32), pltpu.VMEM((NODES, D), BF), pltpu.SemaphoreType.DMA((3,))],
        )
    )


def solution(mesh):
    split = Mesh(mesh.devices.reshape(XS, 2, 8, 8), ALL)
    rows = P(ALL, None)
    in_specs = (rows, rows, rows, P(ALL), rows, P(), P(), rows)
    out_specs = (P(), P(), rows)
    return jax.shard_map(local, mesh=split, in_specs=in_specs, out_specs=out_specs, check_vma=False)
```
